512 devices in a mesh: seq: 64 (over x, z_hi, y, core), head: 8 (over z_lo).
Axes of the slice: x: 4, y: 4, z: 16 (z_hi: 2, z_lo: 8; z = z_hi * 8 + z_lo), core: 2. Of those that a mesh axis runs over, the one named last changes fastest.
Arguments:
- queries: bfloat16 [64, 256, 16384], P('head', 'seq'), may hold values from -6 to 6
- keys: bfloat16 [64, 256, 1024], P('head', 'seq'), may hold values from -6 to 6
- values: bfloat16 [64, 256, 1024], P('head', 'seq'), may hold values from -6 to 6
- links: int32 [64, 6], replicated, may hold values from 0 to 63, as said below
Outputs:
- attended: bfloat16 [64, 256, 16384], P('head', 'seq')
The draws below stay inside these ranges and needn't reach their ends.
Inputs may be any that keep to these rules, and one draw needn't show every extreme that they name: For i >= 1, links[i, 0] = i - 1; every entry in slot k of row i is either i - 2 ** k or i; in the last row every slot k < 5 with 2 ** k < 64 holds 64 - 1 - 2 ** k, and slot 5 holds 63.
All inputs are finite; a program needn't handle non-finite values.
Results may differ from the reference program's by a relative error of at most 0.0095.
Values may be sent and summed in bfloat16 or wider, within the bound.
No kernel may reach another device: no remote copies, remote signals or barrier semaphores. Data moves between devices by JAX's collectives and lax.ppermute only.
A program may use at most 128 MiB of HBM per device.

```python
import jax
import jax.numpy as jnp
from jax import lax

QH = 128
KVH = 8
HD = 128
RLEN = 256
LINKS = 6
RESP = 64


def draw_queries(key, part):
    key = jax.random.fold_in(key, 11)
    base = jnp.clip(jax.random.normal(key, (RESP, RLEN, QH * HD), jnp.float32), -6.0, 6.0)
    return base.astype(jnp.bfloat16)


def draw_keys(key, part):
    key = jax.random.fold_in(key, 23)
    base = jnp.clip(jax.random.normal(key, (RESP, RLEN, KVH * HD), jnp.float32), -6.0, 6.0)
    return base.astype(jnp.bfloat16)


def draw_links(key, part):
    key = jax.random.fold_in(key, 37)
    response = jnp.arange(RESP, dtype=jnp.int32)[:, None]
    slot = jnp.arange(LINKS, dtype=jnp.int32)[None, :]
    distance = (2 ** slot).astype(jnp.int32)
    raw = jax.random.randint(key, (RESP, LINKS), 0, 1048576, dtype=jnp.int32)
    target = response - distance
    live = (target >= 0) & ((slot == 0) | (raw % (RESP - 1) < response))
    closing = (response == RESP - 1) & (slot == LINKS - 1)
    live = live & jnp.logical_not(closing)
    return jnp.where(live, target, response).astype(jnp.int32)


def shard_levels(stream_key, shape, pieces, least, high):
    factor_of, own = 1.0, jax.random.fold_in(stream_key, 6)
    for dim, blocks in pieces:
        draws = jnp.exp(jax.random.uniform(jax.random.fold_in(own, dim), (blocks,), jnp.float32, least / len(pieces), high / len(pieces)))
        factor_of = factor_of * jnp.repeat(draws, shape[dim] // blocks).reshape([-1 if axis == dim else 1 for axis in range(len(shape))])
    return factor_of


def bell_draw(rng, dims, scale, bound, cuts=(), kind=jnp.bfloat16):
    values = jax.random.normal(rng, dims, jnp.float32) * scale
    if len(cuts) > 0:
        values = shard_levels(rng, dims, cuts, -0.22, 0.18) * values
    return jnp.clip(values, min=-bound, max=bound).astype(kind)


def setup_inputs(seed: int = 0) -> dict:
    splits = jax.random.split(jax.random.key(seed), 5)
    queries = draw_queries(jax.random.fold_in(splits[4], 71), 0)
    keys = draw_keys(jax.random.fold_in(splits[4], 71), 0)
    values = bell_draw(splits[2], (RESP, RLEN, KVH * HD), 1.0, 6.0, ((0, 8), (1, 64)))
    links = draw_links(jax.random.fold_in(splits[4], 71), 0)
    return {"queries": queries, "keys": keys, "values": values, "links": links}


def reference(queries, keys, values, links):
    scale = HD ** -0.5
    repeat = QH // KVH
    qall = queries.reshape(RESP, RLEN, KVH, repeat, HD)
    kall = keys.reshape(RESP, RLEN, KVH, HD)
    vall = values.reshape(RESP, RLEN, KVH, HD)
    slots = jnp.arange(LINKS)
    earlier = slots[:, None] > slots[None, :]
    qpos = jnp.arange(RLEN)

    def one(index):
        row = links[index].astype(jnp.int32)
        twin = jnp.any((row[:, None] == row[None, :]) & earlier, axis=1)
        valid = (row < index) & jnp.logical_not(twin)
        blocks = jnp.concatenate([index[None].astype(jnp.int32), row]).astype(jnp.int32)
        kblk = kall[blocks].reshape((LINKS + 1) * RLEN, KVH, HD).astype(jnp.float32)
        vblk = vall[blocks].reshape((LINKS + 1) * RLEN, KVH, HD).astype(jnp.float32)
        own = qpos[None, :] <= qpos[:, None]
        cross = jnp.broadcast_to(valid[None, :, None], (RLEN, LINKS, RLEN)).reshape(RLEN, LINKS * RLEN)
        allowed = jnp.concatenate([own, cross], axis=1)
        qrow = qall[index].astype(jnp.float32)
        scores = jnp.einsum("qgrd,kgd->grqk", qrow, kblk) * scale
        scores = jnp.where(allowed[None, None], scores, -1e30)
        peak = jnp.max(scores, axis=-1, keepdims=True)
        weights = jnp.where(allowed[None, None], jnp.exp(scores - peak), 0.0)
        total = jnp.sum(weights, axis=-1)
        rounded = weights.astype(jnp.bfloat16).astype(jnp.float32)
        summed = jnp.einsum("grqk,kgd->grqd", rounded, vblk)
        result = summed / total[..., None]
        return jnp.transpose(result, (2, 0, 1, 3)).reshape(RLEN, QH * HD).astype(jnp.bfloat16)

    return lax.map(one, jnp.arange(RESP, dtype=jnp.int32))
```

```python
import functools
import math

import jax
import jax.numpy as jnp
from jax import lax
from jax.experimental import pallas as pl
from jax.experimental.pallas import tpu as pltpu
from jax.sharding import Mesh, PartitionSpec as P

HD = 128
SLOTS = 6
FACTOR = HD ** (-0.5) * math.log2(math.e)
CHUNK = 512
PLANE = ("x", "y", "c")
OWN, ONE, TWO, EIGHT, SIXTEEN, THIRTYTWO = 0, 2, 4, 6, 8, 10
SOURCES = (
    (ONE, TWO, EIGHT + 1, EIGHT, SIXTEEN, THIRTYTWO),
    (ONE + 1, TWO + 1, OWN, EIGHT + 1, SIXTEEN + 1, THIRTYTWO + 1),
)


def attend_kernel(live_ref, place_ref, q_ref, own_ref, one_ref, two_ref, *refs):
    halves = refs[:6]
    o_ref, k_all, v_all, s_all, peak, acc = refs[6:]
    half_keys = k_all.shape[1] // 2
    keys = 2 * half_keys
    zh, x = place_ref[0], place_ref[1]
    v_all[:, :, HD:] = jnp.ones((v_all.shape[0], keys, HD), jnp.bfloat16)

    def keep(index, half, key_block, value_block):
        at = half * half_keys
        k_all[index, at : at + half_keys, :] = key_block
        v_all[index, at : at + half_keys, :HD] = value_block

    for half in range(2):
        for m in range(2):
            keep(OWN + m, half, own_ref[half, 0, m], own_ref[half, 1, m])
            keep(ONE + jnp.where(x < 1, 1 - m, m), half, one_ref[m, half, 0], one_ref[m, half, 1])
            keep(TWO + jnp.where(x < 2, 1 - m, m), half, two_ref[m, half, 0], two_ref[m, half, 1])
            for place, pair in ((EIGHT, 0), (SIXTEEN, 2), (THIRTYTWO, 4)):
                keep(place + m, half, halves[pair + half][0, m], halves[pair + half][1, m])

    sources = q_ref.shape[0]
    per = q_ref.shape[2]
    step_sources = CHUNK // per

    def scores_of(query, index):
        return (
            lax.dot_general(
                query, k_all[index], (((1,), (1,)), ((), ())), preferred_element_type=jnp.float32
            )
            * FACTOR
        )

    def sums_of(slot, index):
        top = peak[...]
        shifted = s_all[slot] - jnp.concatenate([top] * (keys // HD), axis=1)
        return jnp.dot(
            jnp.exp2(shifted).astype(jnp.bfloat16), v_all[index], preferred_element_type=jnp.float32
        )

    def widest(scores):
        return functools.reduce(
            jnp.maximum, [scores[:, at : at + HD] for at in range(0, keys, HD)]
        )

    key = lax.broadcasted_iota(jnp.int32, (1, keys), 1)
    inner = key % half_keys
    key_half = jnp.where(key < half_keys, zh, 1 - zh)
    key_pos = (inner // 32) * 64 + key_half * 32 + inner % 32

    for m in range(2):

        def chunk(step, carry, m=m):
            start = step * step_sources
            query = q_ref[pl.ds(start, step_sources), m].reshape(CHUNK, HD)
            row = lax.broadcasted_iota(jnp.int32, (CHUNK, 1), 0)
            source = start + row // per
            query_pos = (source // 8) * 64 + zh * 32 + (source % 8) * 4 + row % 4
            scores = jnp.where(key_pos <= query_pos, scores_of(query, OWN + m), -1e30)
            s_all[0] = scores
            peak[...] = widest(scores)
            for slot, index in enumerate(SOURCES[m]):

                @pl.when(live_ref[m, slot] != 0)
                def _(slot=slot, index=index):
                    scores = scores_of(query, index)
                    s_all[slot + 1] = scores
                    peak[...] = jnp.maximum(peak[...], widest(scores))

            peak[...] = jnp.broadcast_to(jnp.max(peak[...], axis=1, keepdims=True), (CHUNK, HD))
            acc[...] = sums_of(0, OWN + m)
            for slot, index in enumerate(SOURCES[m]):

                @pl.when(live_ref[m, slot] != 0)
                def _(slot=slot, index=index):
                    acc[...] += sums_of(slot + 1, index)

            result = (acc[:, :HD] / acc[:, HD:]).astype(jnp.bfloat16)
            o_ref[pl.ds(start, step_sources), m] = result.reshape(step_sources, per, HD)
            return carry

        lax.fori_loop(0, sources // step_sources, chunk, 0)


def attend(live, place, query, own, one, two, halves):
    keys = 2 * own.shape[3]
    smem = pl.BlockSpec(memory_space=pltpu.SMEM)
    vmem = pl.BlockSpec(memory_space=pltpu.VMEM)
    return pl.pallas_call(
        attend_kernel,
        out_shape=jax.ShapeDtypeStruct(query.shape, jnp.bfloat16),
        in_specs=[smem, smem] + [vmem] * (4 + len(halves)),
        out_specs=vmem,
        scratch_shapes=[
            pltpu.VMEM((12, keys, HD), jnp.bfloat16),
            pltpu.VMEM((12, keys, 2 * HD), jnp.bfloat16),
            pltpu.VMEM((SLOTS + 1, CHUNK, keys), jnp.float32),
            pltpu.VMEM((CHUNK, HD), jnp.float32),
            pltpu.VMEM((CHUNK, 2 * HD), jnp.float32),
        ],
        compiler_params=pltpu.CompilerParams(vmem_limit_bytes=40 * 1024 * 1024),
    )(live, place, query, own, one, two, *halves)


def ring(value, by, keep=lambda h: True):
    pairs = [(z, (z + by) % 16) for z in range(16) if keep(z % 8)]
    return lax.ppermute(value, ("zh", "h"), pairs)


def along(value, by):
    return ring(value, by, lambda h: h + by < 8)


def across(value, by, rises):
    pairs = []
    for x in range(4):
        for h in range(8):
            to = h + 1 if rises and x + by >= 4 else h
            if to < 8:
                pairs.append((x * 8 + h, (x + by) % 4 * 8 + to))
    return lax.ppermute(value, ("x", "h"), pairs)


def local(queries, keys, values, links):
    resp, near, width = queries.shape
    groups = keys.shape[2] // HD
    repeat = width // keys.shape[2]
    x, zh, h = lax.axis_index("x"), lax.axis_index("zh"), lax.axis_index("h")

    with jax.named_scope("key_value_exchange"):
        pairs = jnp.stack([keys, values]).reshape(2, 2, 4, near, groups, HD)
        pairs = pairs.transpose(2, 4, 0, 1, 3, 5).reshape(4 * groups, 2, 2, near, HD)
        pairs = lax.all_to_all(pairs, PLANE, split_axis=0, concat_axis=0, tiled=True)
        pairs = pairs.transpose(1, 2, 0, 3, 4).reshape(2, 2, 4 * groups * near, HD)
    with jax.named_scope("query_exchange"):
        packed = queries.reshape(2, 4, near, groups, repeat, HD).transpose(1, 3, 0, 4, 2, 5)
        packed = packed.reshape(4 * groups, 2, repeat * near, HD)
        query = lax.all_to_all(packed, PLANE, split_axis=0, concat_axis=0, tiled=True)
    with jax.named_scope("key_value_spread"):
        above = ring(pairs, -4)
        below = along(pairs, 4)
        eight = along(pairs, 1)
        sixteen = along(pairs, 2)
        other = ring(above, -4)
        pairs, other, above, below, eight, sixteen = lax.optimization_barrier(
            (pairs, other, above, below, eight, sixteen)
        )
        own = jnp.stack([pairs, other])
        blocks = own.transpose(2, 0, 1, 3, 4)
        one = jnp.stack([across(blocks[0], 1, False), across(blocks[1], 1, True)])
        two = jnp.stack([across(blocks[0], 2, False), across(blocks[1], 2, True)])
        halves = (eight, along(other, 1), sixteen, along(other, 2), below, above)
    with jax.named_scope("attend"):
        place = jnp.stack([zh, x]).astype(jnp.int32)
        index = h * resp + x + 4 * jnp.arange(2)
        live = (links[index] != index[:, None]).astype(jnp.int32)
        result = attend(live, place, query, own, one, two, halves)
    with jax.named_scope("return_exchange"):
        result = lax.all_to_all(result, PLANE, split_axis=0, concat_axis=0, tiled=True)
        result = result.reshape(4, groups, 2, repeat, near, HD).transpose(2, 0, 4, 1, 3, 5)
        return result.reshape(resp, near, width)


def solution(mesh):
    fine = Mesh(mesh.devices.reshape(4, 2, 4, 2, 8), ("x", "zh", "y", "c", "h"))
    placed = P("h", ("x", "zh", "y", "c"), None)
    return jax.shard_map(
        local, mesh=fine, in_specs=(placed, placed, placed, P()), out_specs=placed, check_vma=False
    )
```

```python
import functools
import math

import jax
import jax.numpy as jnp
from jax import lax
from jax.experimental import pallas as pl
from jax.experimental.pallas import tpu as pltpu
from jax.sharding import Mesh, PartitionSpec as P

HD = 128
SLOTS = 6
FACTOR = HD ** (-0.5) * math.log2(math.e)
CHUNK = 1024
SAFE_CHUNK = 512
LEAST, MOST = 2.0**-60, 2.0**60
PLANE = ("x", "y", "c")
OWN, ONE, TWO, EIGHT, SIXTEEN, THIRTYTWO = 0, 2, 4, 6, 8, 10
SOURCES = (
    (ONE + 1, ONE, TWO, EIGHT, SIXTEEN, THIRTYTWO),
    (OWN, ONE + 1, TWO + 1, EIGHT + 1, SIXTEEN + 1, THIRTYTWO + 1),
)


def scores_of(query, key_block):
    dims = (((1,), (1,)), ((), ()))
    return lax.dot_general(query, key_block, dims, preferred_element_type=jnp.float32) * FACTOR


def causal(start, count, per, zh, half_keys):
    key = lax.broadcasted_iota(jnp.int32, (1, 2 * half_keys), 1)
    inner = key % half_keys
    key_half = jnp.where(key < half_keys, zh, 1 - zh)
    key_pos = (inner // 32) * 64 + key_half * 32 + inner % 32
    row = lax.broadcasted_iota(jnp.int32, (count, 1), 0)
    source = start + row // per
    query_pos = (source // 8) * 64 + zh * 32 + (source % 8) * 4 + row % 4
    return key_pos <= query_pos


def place_block(k_some, v_some, at, block, m, live):
    half_keys = block.shape[3]
    keys = 2 * half_keys
    for half in range(2):
        columns = slice(half * half_keys, (half + 1) * half_keys)
        k_some[at, :, columns] = block[half, 0, m].T
        rows = slice(at * keys + half * half_keys, at * keys + (half + 1) * half_keys)
        ones = jnp.ones((half_keys, HD), jnp.bfloat16)
        value_block = block[half, 1, m]
        if live is not None:
            alive = jnp.where(live != 0, 1.0, 0.0) > 0
            value_block = jnp.where(alive, value_block, jnp.zeros_like(value_block))
            ones = jnp.where(alive, ones, jnp.zeros_like(ones))
        v_some[rows, :HD] = value_block
        v_some[rows, HD:] = ones


def weighted(query, k_some, v_some, first, count, allowed):
    keys = k_some.shape[2]
    parts = []
    for at in range(first, first + count):
        scores = jnp.dot(query, k_some[at], preferred_element_type=jnp.float32)
        weights = jnp.exp2(scores * FACTOR)
        if allowed is not None and at == first:
            weights = jnp.where(allowed, weights, 0.0)
        parts.append(weights.astype(jnp.bfloat16))
    values = v_some[first * keys : (first + count) * keys, :]
    return jnp.dot(jnp.concatenate(parts, axis=1), values, preferred_element_type=jnp.float32)


def early_kernel(live_ref, place_ref, q_ref, own, o_ref, k_some, v_some):
    zh = place_ref[0]
    place_block(k_some, v_some, 0, own, 0, None)
    place_block(k_some, v_some, 1, own, 1, None)
    place_block(k_some, v_some, 2, own, 0, live_ref[1, 0])
    per = q_ref.shape[2]
    step_sources = CHUNK // per
    for m in range(2):

        def chunk(step, carry, m=m):
            start = step * step_sources
            query = q_ref[pl.ds(start, step_sources), m].reshape(CHUNK, HD)
            allowed = causal(start, CHUNK, per, zh, own.shape[3])
            total = weighted(query, k_some, v_some, m, 1 + m, allowed)
            o_ref[pl.ds(start, step_sources), m] = total.reshape(step_sources, per, 2 * HD)
            return carry

        lax.fori_loop(0, q_ref.shape[0] // step_sources, chunk, 0)


def late_kernel(live_ref, place_ref, q_ref, early_ref, *refs):
    blocks = refs[:6]
    o_ref, k_some, v_some, k_all, v_all, s_all, peak, acc, bad_ref = refs[6:]
    own, one, two, eight, sixteen, thirtytwo = blocks
    zh = place_ref[0]
    half_keys = own.shape[3]
    keys = 2 * half_keys
    per = q_ref.shape[2]
    firsts, counts = (0, 6), (6, 5)
    for m in range(2):
        sets = [(one, 1, m), (two, m, 2), (eight, m, 3), (sixteen, m, 4), (thirtytwo, m, 5)]
        if m == 0:
            sets.append((one, 0, 1))
        for at, (block, which, slot) in enumerate(sets):
            place_block(k_some, v_some, firsts[m] + at, block, which, live_ref[m, slot])
    bad_ref[...] = jnp.zeros_like(bad_ref)

    for m in range(2):
        step_sources = CHUNK // per

        def quick(step, carry, m=m):
            start = step * step_sources
            query = q_ref[pl.ds(start, step_sources), m].reshape(CHUNK, HD)
            total = early_ref[pl.ds(start, step_sources), m].reshape(CHUNK, 2 * HD)
            total += weighted(query, k_some, v_some, firsts[m], counts[m], None)
            summed = total[:, HD:]
            fine = (summed >= LEAST) & (summed <= MOST)
            result = (total[:, :HD] / summed).astype(jnp.bfloat16)
            o_ref[pl.ds(start, step_sources), m] = result.reshape(step_sources, per, HD)
            bad = jnp.where(fine, 0.0, 1.0)
            bad_ref[...] = jnp.maximum(bad_ref[...], jnp.max(bad.reshape(-1, 8, HD), axis=0))
            return carry

        lax.fori_loop(0, q_ref.shape[0] // step_sources, quick, 0)

    @pl.when(jnp.max(bad_ref[...]) > 0.0)
    def _():
        v_all[:, :, HD:] = jnp.ones((v_all.shape[0], keys, HD), jnp.bfloat16)
        for place, block in zip((OWN, ONE, TWO, EIGHT, SIXTEEN, THIRTYTWO), blocks):
            for m in range(2):
                for half in range(2):
                    rows = slice(half * half_keys, (half + 1) * half_keys)
                    k_all[place + m, rows, :] = block[half, 0, m]
                    v_all[place + m, rows, :HD] = block[half, 1, m]
        step_sources = SAFE_CHUNK // per

        def sums_of(slot, index):
            top = peak[...]
            shifted = s_all[slot] - jnp.concatenate([top] * (keys // HD), axis=1)
            return jnp.dot(
                jnp.exp2(shifted).astype(jnp.bfloat16),
                v_all[index],
                preferred_element_type=jnp.float32,
            )

        def widest(scores):
            return functools.reduce(
                jnp.maximum, [scores[:, at : at + HD] for at in range(0, keys, HD)]
            )

        for m in range(2):

            def chunk(step, carry, m=m):
                start = step * step_sources
                query = q_ref[pl.ds(start, step_sources), m].reshape(SAFE_CHUNK, HD)
                allowed = causal(start, SAFE_CHUNK, per, zh, half_keys)
                scores = jnp.where(allowed, scores_of(query, k_all[OWN + m]), -1e30)
                s_all[0] = scores
                peak[...] = widest(scores)
                for slot, index in enumerate(SOURCES[m]):

                    @pl.when(live_ref[m, slot] != 0)
                    def _(slot=slot, index=index):
                        scores = scores_of(query, k_all[index])
                        s_all[slot + 1] = scores
                        peak[...] = jnp.maximum(peak[...], widest(scores))

                top = jnp.max(peak[...], axis=1, keepdims=True)
                peak[...] = jnp.broadcast_to(top, (SAFE_CHUNK, HD))
                acc[...] = sums_of(0, OWN + m)
                for slot, index in enumerate(SOURCES[m]):

                    @pl.when(live_ref[m, slot] != 0)
                    def _(slot=slot, index=index):
                        acc[...] += sums_of(slot + 1, index)

                result = (acc[:, :HD] / acc[:, HD:]).astype(jnp.bfloat16)
                o_ref[pl.ds(start, step_sources), m] = result.reshape(step_sources, per, HD)
                return carry

            lax.fori_loop(0, q_ref.shape[0] // step_sources, chunk, 0)


def call(kernel, outputs, scratch, blocks, scalars, arrays):
    smem = pl.BlockSpec(memory_space=pltpu.SMEM)
    vmem = pl.BlockSpec(memory_space=pltpu.VMEM)
    rows = 4096
    return pl.pallas_call(
        kernel,
        out_shape=outputs,
        in_specs=[smem] * len(scalars) + [vmem] * len(arrays),
        out_specs=vmem,
        scratch_shapes=scratch,
        compiler_params=pltpu.CompilerParams(vmem_limit_bytes=44 * 1024 * 1024),
        cost_estimate=pl.CostEstimate(
            flops=int(rows * blocks * 256 * HD * 6),
            bytes_accessed=8 * 1024 * 1024,
            transcendentals=int(rows * blocks * 256),
        ),
    )(*scalars, *arrays)


def block_scratch(count, keys):
    return [
        pltpu.VMEM((count, HD, keys), jnp.bfloat16),
        pltpu.VMEM((count * keys, 2 * HD), jnp.bfloat16),
    ]


def attend_early(live, place, query, own):
    keys = 2 * own.shape[3]
    output = jax.ShapeDtypeStruct(query.shape[:3] + (2 * HD,), jnp.float32)
    return call(early_kernel, output, block_scratch(3, keys), 1.5, (live, place), (query, own))


def attend_late(live, place, query, early, *blocks):
    keys = 2 * blocks[0].shape[3]
    output = jax.ShapeDtypeStruct(query.shape, jnp.bfloat16)
    scratch = block_scratch(11, keys) + [
        pltpu.VMEM((12, keys, HD), jnp.bfloat16),
        pltpu.VMEM((12, keys, 2 * HD), jnp.bfloat16),
        pltpu.VMEM((SLOTS + 1, SAFE_CHUNK, keys), jnp.float32),
        pltpu.VMEM((SAFE_CHUNK, HD), jnp.float32),
        pltpu.VMEM((SAFE_CHUNK, 2 * HD), jnp.float32),
        pltpu.VMEM((8, HD), jnp.float32),
    ]
    return call(late_kernel, output, scratch, 5.5, (live, place), (query, early) + blocks)


def ring(value, by, keep=lambda h: True):
    pairs = [(z, (z + by) % 16) for z in range(16) if keep(z % 8)]
    return lax.ppermute(value, ("zh", "h"), pairs)


def along(value, by):
    return ring(value, by, lambda h: h + by < 8)


def across(value, by):
    pairs = []
    for x in range(4):
        for h in range(8):
            to = h + (x + by) // 4
            if to < 8:
                pairs.append((x * 8 + h, (x + by) % 4 * 8 + to))
    return lax.ppermute(value, ("x", "h"), pairs)


def local(queries, keys, values, links):
    resp, near, width = queries.shape
    groups = keys.shape[2] // HD
    repeat = width // keys.shape[2]
    x, zh, h = lax.axis_index("x"), lax.axis_index("zh"), lax.axis_index("h")

    with jax.named_scope("key_value_exchange"):
        pairs = jnp.stack([keys, values]).reshape(2, 4, 2, near, groups, HD)
        pairs = pairs.transpose(1, 4, 0, 2, 3, 5).reshape(4 * groups, 2, 2, near, HD)
        pairs = lax.all_to_all(pairs, PLANE, split_axis=0, concat_axis=0, tiled=True)
        pairs = pairs.transpose(1, 2, 0, 3, 4).reshape(2, 2, 4 * groups * near, HD)
    with jax.named_scope("other_half"):
        own = jnp.stack([pairs, ring(pairs, 8)])
    with jax.named_scope("query_exchange"):
        packed = queries.reshape(4, 2, near, groups, repeat, HD).transpose(0, 3, 1, 4, 2, 5)
        packed = packed.reshape(4 * groups, 2, repeat * near, HD)
        query = lax.all_to_all(packed, PLANE, split_axis=0, concat_axis=0, tiled=True)
    with jax.named_scope("key_value_spread"):
        thirtytwo = ring(own, -4, lambda h: h < 4)
        sixteen = along(own, 2)
        two = across(own, 2)
        one = across(own, 1)
        eight = along(own, 1)
    with jax.named_scope("attend"):
        place = jnp.stack([zh, x]).astype(jnp.int32)
        index = h * resp + 2 * x + jnp.arange(2)
        live = (links[index] != index[:, None]).astype(jnp.int32)
        early = attend_early(live, place, query, own)
        result = attend_late(live, place, query, early, own, one, two, eight, sixteen, thirtytwo)
    with jax.named_scope("return_exchange"):
        result = lax.all_to_all(result, PLANE, split_axis=0, concat_axis=0, tiled=True)
        result = result.reshape(4, groups, 2, repeat, near, HD).transpose(0, 2, 4, 1, 3, 5)
        return result.reshape(resp, near, width)


def solution(mesh):
    fine = Mesh(mesh.devices.reshape(4, 2, 4, 2, 8), ("x", "zh", "y", "c", "h"))
    placed = P("h", ("x", "zh", "y", "c"), None)
    return jax.shard_map(
        local, mesh=fine, in_specs=(placed, placed, placed, P()), out_specs=placed, check_vma=False
    )
```

```python
import functools
import math

import jax
import jax.numpy as jnp
from jax import lax
from jax.experimental import pallas as pl
from jax.experimental.pallas import tpu as pltpu
from jax.sharding import Mesh, PartitionSpec as P

HD = 128
SLOTS = 6
FACTOR = HD ** (-0.5) * math.log2(math.e)
CHUNK = 1024
SAFE_CHUNK = 512
LEAST, MOST = 2.0**-60, 2.0**60
PLANE = ("x", "y", "c")
OWN, ONE, TWO, EIGHT, SIXTEEN, THIRTYTWO = 0, 2, 4, 6, 8, 10
SOURCES = (
    (ONE + 1, ONE, TWO, EIGHT, SIXTEEN, THIRTYTWO),
    (OWN, ONE + 1, TWO + 1, EIGHT + 1, SIXTEEN + 1, THIRTYTWO + 1),
)


def scores_of(query, key_block):
    dims = (((1,), (1,)), ((), ()))
    return lax.dot_general(query, key_block, dims, preferred_element_type=jnp.float32) * FACTOR


def causal(start, count, per, zh, keys):
    key_pos = lax.broadcasted_iota(jnp.int32, (1, keys), 1)
    row = lax.broadcasted_iota(jnp.int32, (count, 1), 0)
    source = start + row // per
    query_pos = (source // 8) * 64 + zh * 32 + (source % 8) * 4 + row % 4
    return key_pos <= query_pos


def place_block(k_some, v_some, at, block, m, live):
    keys = block.shape[2]
    k_some[at] = block[0, m].T
    rows = slice(at * keys, (at + 1) * keys)
    ones = jnp.ones((keys, HD), jnp.bfloat16)
    value_block = block[1, m]
    if live is not None:
        alive = jnp.where(live != 0, 1.0, 0.0) > 0
        value_block = jnp.where(alive, value_block, jnp.zeros_like(value_block))
        ones = jnp.where(alive, ones, jnp.zeros_like(ones))
    v_some[rows, :HD] = value_block
    v_some[rows, HD:] = ones


def weighted(query, k_some, v_some, first, count, allowed):
    keys = k_some.shape[2]
    parts = []
    for at in range(first, first + count):
        scores = jnp.dot(query, k_some[at], preferred_element_type=jnp.float32)
        weights = jnp.exp2(scores * FACTOR)
        if allowed is not None and at == first:
            weights = jnp.where(allowed, weights, 0.0)
        parts.append(weights.astype(jnp.bfloat16))
    values = v_some[first * keys : (first + count) * keys, :]
    return jnp.dot(jnp.concatenate(parts, axis=1), values, preferred_element_type=jnp.float32)


def prepare_kernel(live_ref, own, k_some, v_some):
    place_block(k_some, v_some, 0, own, 0, None)
    place_block(k_some, v_some, 1, own, 1, None)
    place_block(k_some, v_some, 2, own, 0, live_ref[1, 0])


def early_kernel(place_ref, q_ref, k_some, v_some, o_ref):
    per = q_ref.shape[2]
    step_sources = CHUNK // per
    for m in range(2):

        def chunk(step, carry, m=m):
            start = step * step_sources
            query = q_ref[pl.ds(start, step_sources), m].reshape(CHUNK, HD)
            allowed = causal(start, CHUNK, per, place_ref[0], k_some.shape[2])
            total = weighted(query, k_some, v_some, m, 1 + m, allowed)
            o_ref[pl.ds(start, step_sources), m] = total.reshape(step_sources, per, 2 * HD)
            return carry

        lax.fori_loop(0, q_ref.shape[0] // step_sources, chunk, 0)


def middle_kernel(live_ref, q_ref, early_ref, eight, sixteen, o_ref, k_some, v_some):
    per = q_ref.shape[2]
    step_sources = CHUNK // per
    for m in range(2):
        place_block(k_some, v_some, 2 * m, eight, m, live_ref[m, 3])
        place_block(k_some, v_some, 2 * m + 1, sixteen, m, live_ref[m, 4])
    for m in range(2):

        def chunk(step, carry, m=m):
            start = step * step_sources
            query = q_ref[pl.ds(start, step_sources), m].reshape(CHUNK, HD)
            total = early_ref[pl.ds(start, step_sources), m].reshape(CHUNK, 2 * HD)
            total += weighted(query, k_some, v_some, 2 * m, 2, None)
            o_ref[pl.ds(start, step_sources), m] = total.reshape(step_sources, per, 2 * HD)
            return carry

        lax.fori_loop(0, q_ref.shape[0] // step_sources, chunk, 0)


def late_kernel(live_ref, place_ref, q_ref, early_ref, *refs):
    blocks = refs[:6]
    o_ref, k_some, v_some, k_all, v_all, s_all, peak, acc, bad_ref = refs[6:]
    own, one, two, eight, sixteen, thirtytwo = blocks
    zh = place_ref[0]
    keys = own.shape[2]
    per = q_ref.shape[2]
    firsts, counts = (0, 4), (4, 3)
    for m in range(2):
        sets = [(one, 1, m), (two, m, 2), (thirtytwo, m, 5)]
        if m == 0:
            sets.append((one, 0, 1))
        for at, (block, which, slot) in enumerate(sets):
            place_block(k_some, v_some, firsts[m] + at, block, which, live_ref[m, slot])
    bad_ref[...] = jnp.zeros_like(bad_ref)

    for m in range(2):
        step_sources = CHUNK // per

        def quick(step, carry, m=m):
            start = step * step_sources
            query = q_ref[pl.ds(start, step_sources), m].reshape(CHUNK, HD)
            total = early_ref[pl.ds(start, step_sources), m].reshape(CHUNK, 2 * HD)
            total += weighted(query, k_some, v_some, firsts[m], counts[m], None)
            summed = total[:, HD:]
            fine = (summed >= LEAST) & (summed <= MOST)
            result = (total[:, :HD] / summed).astype(jnp.bfloat16)
            o_ref[pl.ds(start, step_sources), m] = result.reshape(step_sources, per, HD)
            bad = jnp.where(fine, 0.0, 1.0)
            bad_ref[...] = jnp.maximum(bad_ref[...], jnp.max(bad.reshape(-1, 8, HD), axis=0))
            return carry

        lax.fori_loop(0, q_ref.shape[0] // step_sources, quick, 0)

    @pl.when(jnp.max(bad_ref[...]) > 0.0)
    def _():
        v_all[:, :, HD:] = jnp.ones((v_all.shape[0], keys, HD), jnp.bfloat16)
        for place, block in zip((OWN, ONE, TWO, EIGHT, SIXTEEN, THIRTYTWO), blocks):
            for m in range(2):
                k_all[place + m] = block[0, m]
                v_all[place + m, :, :HD] = block[1, m]
        step_sources = SAFE_CHUNK // per

        def sums_of(slot, index):
            top = peak[...]
            shifted = s_all[slot] - jnp.concatenate([top] * (keys // HD), axis=1)
            return jnp.dot(
                jnp.exp2(shifted).astype(jnp.bfloat16),
                v_all[index],
                preferred_element_type=jnp.float32,
            )

        def widest(scores):
            return functools.reduce(
                jnp.maximum, [scores[:, at : at + HD] for at in range(0, keys, HD)]
            )

        for m in range(2):

            def chunk(step, carry, m=m):
                start = step * step_sources
                query = q_ref[pl.ds(start, step_sources), m].reshape(SAFE_CHUNK, HD)
                allowed = causal(start, SAFE_CHUNK, per, zh, keys)
                scores = jnp.where(allowed, scores_of(query, k_all[OWN + m]), -1e30)
                s_all[0] = scores
                peak[...] = widest(scores)
                for slot, index in enumerate(SOURCES[m]):

                    @pl.when(live_ref[m, slot] != 0)
                    def _(slot=slot, index=index):
                        scores = scores_of(query, k_all[index])
                        s_all[slot + 1] = scores
                        peak[...] = jnp.maximum(peak[...], widest(scores))

                top = jnp.max(peak[...], axis=1, keepdims=True)
                peak[...] = jnp.broadcast_to(top, (SAFE_CHUNK, HD))
                acc[...] = sums_of(0, OWN + m)
                for slot, index in enumerate(SOURCES[m]):

                    @pl.when(live_ref[m, slot] != 0)
                    def _(slot=slot, index=index):
                        acc[...] += sums_of(slot + 1, index)

                result = (acc[:, :HD] / acc[:, HD:]).astype(jnp.bfloat16)
                o_ref[pl.ds(start, step_sources), m] = result.reshape(step_sources, per, HD)
                return carry

            lax.fori_loop(0, q_ref.shape[0] // step_sources, chunk, 0)


def call(kernel, outputs, scratch, flops, scalars, arrays):
    smem = pl.BlockSpec(memory_space=pltpu.SMEM)
    vmem = pl.BlockSpec(memory_space=pltpu.VMEM)
    return pl.pallas_call(
        kernel,
        out_shape=outputs,
        in_specs=[smem] * len(scalars) + [vmem] * len(arrays),
        out_specs=jax.tree.map(lambda _: vmem, outputs),
        scratch_shapes=scratch,
        compiler_params=pltpu.CompilerParams(vmem_limit_bytes=44 * 1024 * 1024),
        cost_estimate=pl.CostEstimate(flops=flops, bytes_accessed=2**20, transcendentals=0),
    )(*scalars, *arrays)


def block_shapes(count, keys):
    return [(count, HD, keys), (count * keys, 2 * HD)]


def block_scratch(count, keys):
    return [pltpu.VMEM(shape, jnp.bfloat16) for shape in block_shapes(count, keys)]


def attend_prepare(live, own):
    keys = own.shape[2]
    outputs = [jax.ShapeDtypeStruct(shape, jnp.bfloat16) for shape in block_shapes(3, keys)]
    return call(prepare_kernel, outputs, [], 30 * 10**9, (live,), (own,))


def attend_early(place, query, keys_own, values_own):
    output = jax.ShapeDtypeStruct(query.shape[:3] + (2 * HD,), jnp.float32)
    return call(early_kernel, output, [], 4 * 10**9, (place,), (query, keys_own, values_own))


def attend_middle(live, query, early, eight, sixteen):
    output = jax.ShapeDtypeStruct(early.shape, jnp.float32)
    scratch = block_scratch(4, eight.shape[2])
    return call(middle_kernel, output, scratch, 4 * 10**9, (live,), (query, early, eight, sixteen))


def attend_late(live, place, query, early, *blocks):
    keys = blocks[0].shape[2]
    output = jax.ShapeDtypeStruct(query.shape, jnp.bfloat16)
    scratch = block_scratch(7, keys) + [
        pltpu.VMEM((12, keys, HD), jnp.bfloat16),
        pltpu.VMEM((12, keys, 2 * HD), jnp.bfloat16),
        pltpu.VMEM((SLOTS + 1, SAFE_CHUNK, keys), jnp.float32),
        pltpu.VMEM((SAFE_CHUNK, HD), jnp.float32),
        pltpu.VMEM((SAFE_CHUNK, 2 * HD), jnp.float32),
        pltpu.VMEM((8, HD), jnp.float32),
    ]
    return call(late_kernel, output, scratch, 6 * 10**9, (live, place), (query, early) + blocks)


def ring(value, by, keep=lambda h: True):
    pairs = [(z, (z + by) % 16) for z in range(16) if keep(z % 8)]
    return lax.ppermute(value, ("zh", "h"), pairs)


def along(value, by):
    return ring(value, by, lambda h: h + by < 8)


def across(value, by):
    return lax.ppermute(value, "x", [(x, (x + by) % 4) for x in range(4)])


def local(queries, keys, values, links):
    resp, near, width = queries.shape
    groups = keys.shape[2] // HD
    repeat = width // keys.shape[2]
    x, zh, h = lax.axis_index("x"), lax.axis_index("zh"), lax.axis_index("h")

    with jax.named_scope("key_value_exchange"):
        own = jnp.stack([keys, values]).reshape(2, 4, 2, near, groups, HD).transpose(1, 4, 0, 2, 3, 5)
        own = jnp.broadcast_to(own[:, None], (4, 2, groups, 2, 2, near, HD))
        own = own.reshape(8 * groups, 2, 2, near, HD)
        own = lax.all_to_all(own, ("x", "zh", "y", "c"), split_axis=0, concat_axis=0, tiled=True)
        own = own.transpose(1, 2, 0, 3, 4).reshape(2, 2, 8 * groups * near, HD)
    with jax.named_scope("query_exchange"):
        packed = queries.reshape(4, 2, near, groups, repeat, HD).transpose(0, 3, 1, 4, 2, 5)
        packed = packed.reshape(4 * groups, 2, repeat * near, HD)
        query = lax.all_to_all(packed, PLANE, split_axis=0, concat_axis=0, tiled=True)
    place = zh.astype(jnp.int32).reshape(1)
    index = h * resp + 2 * x + jnp.arange(2)
    live = (links[index] != index[:, None]).astype(jnp.int32)
    with jax.named_scope("key_value_spread"):
        eight = along(own, 1)
        thirtytwo = ring(own, -4, lambda h: h < 4)
        sixteen = along(own, 2)
        two = across(jnp.where(x >= 2, eight, own), 2)
        one = across(jnp.where(x >= 3, eight, own), 1)
    with jax.named_scope("attend"):
        query, eight = lax.optimization_barrier((query, eight))
        early = attend_early(place, query, *attend_prepare(live, own))
        early = attend_middle(live, query, early, eight, sixteen)
        result = attend_late(live, place, query, early, own, one, two, eight, sixteen, thirtytwo)
    with jax.named_scope("return_exchange"):
        result = lax.all_to_all(result, PLANE, split_axis=0, concat_axis=0, tiled=True)
        result = result.reshape(4, groups, 2, repeat, near, HD).transpose(0, 2, 4, 1, 3, 5)
        return result.reshape(resp, near, width)


def solution(mesh):
    fine = Mesh(mesh.devices.reshape(4, 2, 4, 2, 8), ("x", "zh", "y", "c", "h"))
    placed = P("h", ("x", "zh", "y", "c"), None)
    return jax.shard_map(
        local, mesh=fine, in_specs=(placed, placed, placed, P()), out_specs=placed, check_vma=False
    )
```

```python
import functools
import math

import jax
import jax.numpy as jnp
from jax import lax
from jax.experimental import pallas as pl
from jax.experimental.pallas import tpu as pltpu
from jax.sharding import Mesh, PartitionSpec as P

HD = 128
SLOTS = 6
FACTOR = HD ** (-0.5) * math.log2(math.e)
CHUNK = 2048
SAFE_CHUNK = 512
LEAST, MOST = 2.0**-60, 2.0**60
PLANE = ("x", "y", "c")
OWN, ONE, TWO, EIGHT, SIXTEEN, THIRTYTWO = 0, 2, 4, 6, 8, 10
SOURCES = (
    (ONE + 1, ONE, TWO, EIGHT, SIXTEEN, THIRTYTWO),
    (OWN, ONE + 1, TWO + 1, EIGHT + 1, SIXTEEN + 1, THIRTYTWO + 1),
)


def scores_of(query, key_block):
    dims = (((1,), (1,)), ((), ()))
    return lax.dot_general(query, key_block, dims, preferred_element_type=jnp.float32) * FACTOR


def causal(start, count, per, zh, keys):
    key = lax.broadcasted_iota(jnp.int32, (1, keys), 1)
    inner = key % (keys // 2)
    key_half = jnp.where(key < keys // 2, zh, 1 - zh)
    key_pos = (inner // 32) * 64 + key_half * 32 + inner % 32
    row = lax.broadcasted_iota(jnp.int32, (count, 1), 0)
    source = start + row // per
    query_pos = (source // 8) * 64 + zh * 32 + (source % 8) * 4 + row % 4
    return key_pos <= query_pos


def weighted(query, total, parts, allowed):
    weights, values = [], []
    for at, (block, which, offset) in enumerate(parts):
        scores = scores_of(query, block[0, which])
        weight = jnp.exp2(scores if offset is None else scores + offset)
        if allowed is not None and at == 0:
            weight = jnp.where(allowed, weight, 0.0)
        weights.append(weight.astype(jnp.bfloat16))
        value_block = block[1, which]
        values.append(jnp.concatenate([value_block, jnp.ones_like(value_block)], axis=1))
    term = jnp.dot(
        jnp.concatenate(weights, axis=1),
        jnp.concatenate(values, axis=0),
        preferred_element_type=jnp.float32,
    )
    return term if total is None else total + term


def live_of(links_ref, place_ref, m, slot):
    index = place_ref[1] + m
    return links_ref[slot, index] != index


def offset_of(links_ref, place_ref, m, slot):
    return jnp.where(live_of(links_ref, place_ref, m, slot), 0.0, -1e30)


def pack_pairs_kernel(keys_ref, values_ref, o_ref, keys, values, sems):
    copies = [
        pltpu.make_async_copy(keys_ref, keys, sems.at[0]),
        pltpu.make_async_copy(values_ref, values, sems.at[1]),
    ]
    for copy in copies:
        copy.start()
    for copy in copies:
        copy.wait()
    groups = keys.shape[2] // HD
    for x in range(4):
        for group in range(groups):
            columns = slice(group * HD, (group + 1) * HD)
            for kind, array in enumerate((keys, values)):
                for m in range(2):
                    piece = array[2 * x + m, :, columns]
                    o_ref[x * groups + group, kind, m] = piece


def join_kernel(mine, other, o_ref):
    half_keys = mine.shape[2]
    o_ref[:, :, :half_keys] = mine[...]
    o_ref[:, :, half_keys:] = other[...]


def pack_queries_kernel(queries, o_ref):
    width = o_ref.shape[3]
    groups = queries.shape[2] // width
    for x in range(4):
        for group in range(groups):
            for m in range(2):
                piece = queries[2 * x + m, :, group * width : (group + 1) * width]
                o_ref[x * groups + group, m] = piece


def early_kernel(links_ref, place_ref, packed, own, eight, sixteen, q_ref, o_ref):
    sources, _, near, width = packed.shape
    per = q_ref.shape[2]
    step_sources = CHUNK // per
    for m in range(2):

        def unpack(source, carry, m=m):
            wide = packed[source, m].astype(jnp.float32)
            rows = [wide[:, at : at + HD] for at in range(0, width, HD)]
            q_ref[source, m] = jnp.concatenate(rows, axis=0).astype(jnp.bfloat16)
            return carry

        lax.fori_loop(0, sources, unpack, 0)
        parts = [(own, m, None)]
        if m == 1:
            parts.append((own, 0, offset_of(links_ref, place_ref, 1, 0)))
        parts.append((eight, m, offset_of(links_ref, place_ref, m, 3)))
        parts.append((sixteen, m, offset_of(links_ref, place_ref, m, 4)))

        def chunk(step, carry, m=m, parts=parts):
            start = step * step_sources
            query = q_ref[pl.ds(start, step_sources), m].reshape(CHUNK, HD)
            allowed = causal(start, CHUNK, per, place_ref[0], own.shape[2])
            total = weighted(query, None, parts, allowed)
            o_ref[pl.ds(start, step_sources), m] = total.reshape(step_sources, per, 2 * HD)
            return carry

        lax.fori_loop(0, sources // step_sources, chunk, 0)


def late_kernel(links_ref, place_ref, q_ref, early_ref, *refs):
    blocks = refs[:6]
    o_ref, k_all, v_all, s_all, peak, acc, bad_ref = refs[6:]
    own, one, two, eight, sixteen, thirtytwo = blocks
    zh = place_ref[0]
    keys = own.shape[2]
    per = q_ref.shape[2]
    bad_ref[...] = jnp.zeros_like(bad_ref)

    for m in range(2):
        step_sources = CHUNK // per
        sets = [(thirtytwo, m, 5), (two, m, 2), (one, 1, m)]
        if m == 0:
            sets.append((one, 0, 1))
        parts = [
            (block, which, offset_of(links_ref, place_ref, m, slot)) for block, which, slot in sets
        ]

        def quick(step, carry, m=m, parts=parts):
            start = step * step_sources
            query = q_ref[pl.ds(start, step_sources), m].reshape(CHUNK, HD)
            total = early_ref[pl.ds(start, step_sources), m].reshape(CHUNK, 2 * HD)
            total = weighted(query, total, parts, None)
            summed = total[:, HD:]
            fine = (summed >= LEAST) & (summed <= MOST)
            result = (total[:, :HD] / summed).astype(jnp.bfloat16)
            o_ref[pl.ds(start, step_sources), m] = result.reshape(step_sources, per, HD)
            bad = jnp.where(fine, 0.0, 1.0)
            bad_ref[...] = jnp.maximum(bad_ref[...], jnp.max(bad.reshape(-1, 8, HD), axis=0))
            return carry

        lax.fori_loop(0, q_ref.shape[0] // step_sources, quick, 0)

    @pl.when(jnp.max(bad_ref[...]) > 0.0)
    def _():
        v_all[:, :, HD:] = jnp.ones((v_all.shape[0], keys, HD), jnp.bfloat16)
        for place, block in zip((OWN, ONE, TWO, EIGHT, SIXTEEN, THIRTYTWO), blocks):
            for m in range(2):
                k_all[place + m] = block[0, m]
                v_all[place + m, :, :HD] = block[1, m]
        step_sources = SAFE_CHUNK // per

        def sums_of(slot, index):
            top = peak[...]
            shifted = s_all[slot] - jnp.concatenate([top] * (keys // HD), axis=1)
            return jnp.dot(
                jnp.exp2(shifted).astype(jnp.bfloat16),
                v_all[index],
                preferred_element_type=jnp.float32,
            )

        def widest(scores):
            return functools.reduce(
                jnp.maximum, [scores[:, at : at + HD] for at in range(0, keys, HD)]
            )

        for m in range(2):

            def chunk(step, carry, m=m):
                start = step * step_sources
                query = q_ref[pl.ds(start, step_sources), m].reshape(SAFE_CHUNK, HD)
                allowed = causal(start, SAFE_CHUNK, per, zh, keys)
                scores = jnp.where(allowed, scores_of(query, k_all[OWN + m]), -1e30)
                s_all[0] = scores
                peak[...] = widest(scores)
                for slot, index in enumerate(SOURCES[m]):

                    @pl.when(live_of(links_ref, place_ref, m, slot))
                    def _(slot=slot, index=index):
                        scores = scores_of(query, k_all[index])
                        s_all[slot + 1] = scores
                        peak[...] = jnp.maximum(peak[...], widest(scores))

                top = jnp.max(peak[...], axis=1, keepdims=True)
                peak[...] = jnp.broadcast_to(top, (SAFE_CHUNK, HD))
                acc[...] = sums_of(0, OWN + m)
                for slot, index in enumerate(SOURCES[m]):

                    @pl.when(live_of(links_ref, place_ref, m, slot))
                    def _(slot=slot, index=index):
                        acc[...] += sums_of(slot + 1, index)

                result = (acc[:, :HD] / acc[:, HD:]).astype(jnp.bfloat16)
                o_ref[pl.ds(start, step_sources), m] = result.reshape(step_sources, per, HD)
                return carry

            lax.fori_loop(0, q_ref.shape[0] // step_sources, chunk, 0)


def call(kernel, outputs, scratch, flops, scalars, arrays):
    smem = pl.BlockSpec(memory_space=pltpu.SMEM)
    vmem = pl.BlockSpec(memory_space=pltpu.VMEM)
    return pl.pallas_call(
        kernel,
        out_shape=outputs,
        in_specs=[smem] * len(scalars) + [vmem] * len(arrays),
        out_specs=jax.tree.map(lambda _: vmem, outputs),
        scratch_shapes=scratch,
        compiler_params=pltpu.CompilerParams(vmem_limit_bytes=44 * 1024 * 1024),
        cost_estimate=pl.CostEstimate(flops=flops, bytes_accessed=2**20, transcendentals=0),
    )(*scalars, *arrays)


def pack_pairs(keys, values):
    resp, near, width = keys.shape
    output = jax.ShapeDtypeStruct((resp // 2 * width // HD, 2, 2, near, HD), jnp.bfloat16)
    block = pltpu.VMEM(keys.shape, keys.dtype)
    return pl.pallas_call(
        pack_pairs_kernel,
        out_shape=output,
        in_specs=[pl.BlockSpec(memory_space=pl.ANY)] * 2,
        out_specs=pl.BlockSpec(memory_space=pltpu.VMEM),
        scratch_shapes=[block, block, pltpu.SemaphoreType.DMA((2,))],
        compiler_params=pltpu.CompilerParams(vmem_limit_bytes=60 * 1024 * 1024),
    )(keys, values)


def join(mine, other):
    shape = mine.shape[:2] + (2 * mine.shape[2], HD)
    output = jax.ShapeDtypeStruct(shape, jnp.bfloat16)
    return call(join_kernel, output, [], 60 * 10**9, (), (mine, other))


def pack_queries(queries, groups):
    resp, near, width = queries.shape
    output = jax.ShapeDtypeStruct((resp // 2 * groups, 2, near, width // groups), jnp.bfloat16)
    return call(pack_queries_kernel, output, [], 10**6, (), (queries,))


def attend_early(links, place, packed, *blocks):
    sources, _, near, width = packed.shape
    shape = (sources, 2, near * width // HD)
    outputs = [
        jax.ShapeDtypeStruct(shape + (HD,), jnp.bfloat16),
        jax.ShapeDtypeStruct(shape + (2 * HD,), jnp.float32),
    ]
    return call(early_kernel, outputs, [], 4 * 10**9, (links, place), (packed,) + blocks)


def attend_late(links, place, query, early, *blocks):
    keys = blocks[0].shape[2]
    output = jax.ShapeDtypeStruct(query.shape, jnp.bfloat16)
    scratch = [
        pltpu.VMEM((12, keys, HD), jnp.bfloat16),
        pltpu.VMEM((12, keys, 2 * HD), jnp.bfloat16),
        pltpu.VMEM((SLOTS + 1, SAFE_CHUNK, keys), jnp.float32),
        pltpu.VMEM((SAFE_CHUNK, HD), jnp.float32),
        pltpu.VMEM((SAFE_CHUNK, 2 * HD), jnp.float32),
        pltpu.VMEM((8, HD), jnp.float32),
    ]
    return call(late_kernel, output, scratch, 6 * 10**9, (links, place), (query, early) + blocks)


def ring(value, by, keep=lambda h: True):
    pairs = [(z, (z + by) % 16) for z in range(16) if keep(z % 8)]
    return lax.ppermute(value, ("zh", "h"), pairs)


def along(value, by):
    return ring(value, by, lambda h: h + by < 8)


def across(value, by):
    return lax.ppermute(value, "x", [(x, (x + by) % 4) for x in range(4)])


def local(queries, keys, values, links):
    resp, near, width = queries.shape
    groups = keys.shape[2] // HD
    repeat = width // keys.shape[2]
    x, zh, h = lax.axis_index("x"), lax.axis_index("zh"), lax.axis_index("h")

    with jax.named_scope("key_value_exchange"):
        own = pack_pairs(keys, values)
        own = lax.all_to_all(own, PLANE, split_axis=0, concat_axis=0, tiled=True)
        own = own.transpose(1, 2, 0, 3, 4).reshape(2, 2, 4 * groups * near, HD)
        own = join(own, ring(own, 8))
    with jax.named_scope("query_exchange"):
        packed = pack_queries(queries, groups)
        packed = lax.all_to_all(packed, PLANE, split_axis=0, concat_axis=0, tiled=True)
    place = jnp.stack([zh, h * resp + 2 * x]).astype(jnp.int32)
    with jax.named_scope("key_value_spread"):
        eight = along(own, 1)
        thirtytwo = ring(own, -4, lambda h: h < 4)
        sixteen = along(own, 2)
        two = across(jnp.where(x >= 2, eight, own), 2)
        one = across(jnp.where(x >= 3, eight, own), 1)
    with jax.named_scope("attend"):
        links = links.T
        query, early = attend_early(links, place, packed, own, eight, sixteen)
        result = attend_late(links, place, query, early, own, one, two, eight, sixteen, thirtytwo)
    with jax.named_scope("return_exchange"):
        result = lax.all_to_all(result, PLANE, split_axis=0, concat_axis=0, tiled=True)
        result = result.reshape(4, groups, 2, repeat, near, HD).transpose(0, 2, 4, 1, 3, 5)
        return result.reshape(resp, near, width)


def solution(mesh):
    fine = Mesh(mesh.devices.reshape(4, 2, 4, 2, 8), ("x", "zh", "y", "c", "h"))
    placed = P("h", ("x", "zh", "y", "c"), None)
    return jax.shard_map(
        local, mesh=fine, in_specs=(placed, placed, placed, P()), out_specs=placed, check_vma=False
    )
```

```python
import functools
import math

import jax
import jax.numpy as jnp
from jax import lax
from jax.experimental import pallas as pl
from jax.experimental.pallas import tpu as pltpu
from jax.sharding import Mesh, PartitionSpec as P

HD = 128
SLOTS = 6
FACTOR = HD ** (-0.5) * math.log2(math.e)
CHUNK = 2048
SAFE_CHUNK = 512
LEAST, MOST = 2.0**-60, 2.0**60
PLANE = ("x", "y", "c")
OWN, ONE, TWO, EIGHT, SIXTEEN, THIRTYTWO = 0, 2, 4, 6, 8, 10
SOURCES = (
    (ONE + 1, ONE, TWO, EIGHT, SIXTEEN, THIRTYTWO),
    (OWN, ONE + 1, TWO + 1, EIGHT + 1, SIXTEEN + 1, THIRTYTWO + 1),
)


def scores_of(query, key_block):
    dims = (((1,), (1,)), ((), ()))
    return lax.dot_general(query, key_block, dims, preferred_element_type=jnp.float32) * FACTOR


def causal(start, count, per, zh, keys):
    key = lax.broadcasted_iota(jnp.int32, (1, keys), 1)
    inner = key % (keys // 2)
    key_half = jnp.where(key < keys // 2, zh, 1 - zh)
    key_pos = (inner // 32) * 64 + key_half * 32 + inner % 32
    row = lax.broadcasted_iota(jnp.int32, (count, 1), 0)
    source = start + row // per
    query_pos = (source // 8) * 64 + zh * 32 + (source % 8) * 4 + row % 4
    return key_pos <= query_pos


def weighted(query, total, parts, allowed):
    weights, values = [], []
    for at, (block, which, offset) in enumerate(parts):
        scores = scores_of(query, block[0, which])
        weight = jnp.exp2(scores if offset is None else scores + offset)
        if allowed is not None and at == 0:
            weight = jnp.where(allowed, weight, 0.0)
        weights.append(weight.astype(jnp.bfloat16))
        value_block = block[1, which]
        values.append(jnp.concatenate([value_block, jnp.ones_like(value_block)], axis=1))
    term = jnp.dot(
        jnp.concatenate(weights, axis=1),
        jnp.concatenate(values, axis=0),
        preferred_element_type=jnp.float32,
    )
    return term if total is None else total + term


def live_of(links_ref, place_ref, m, slot):
    index = place_ref[1] + m
    return links_ref[slot, index] != index


def offset_of(links_ref, place_ref, m, slot):
    return jnp.where(live_of(links_ref, place_ref, m, slot), 0.0, -1e30)


def pack_pairs_kernel(keys_ref, values_ref, o_ref, keys, values, sems):
    copies = [
        pltpu.make_async_copy(keys_ref, keys, sems.at[0]),
        pltpu.make_async_copy(values_ref, values, sems.at[1]),
    ]
    for copy in copies:
        copy.start()
    for copy in copies:
        copy.wait()
    groups = keys.shape[2] // HD
    for x in range(4):
        for group in range(groups):
            columns = slice(group * HD, (group + 1) * HD)
            for kind, array in enumerate((keys, values)):
                for m in range(2):
                    piece = array[2 * x + m, :, columns]
                    o_ref[x * groups + group, kind, m] = piece


def join_kernel(mine, other, o_ref):
    half_keys = mine.shape[2]
    o_ref[:, :, :half_keys] = mine[...]
    o_ref[:, :, half_keys:] = other[...]


def pack_queries_kernel(queries, o_ref):
    groups = o_ref.shape[0] // 4
    width = queries.shape[2] // groups

    def one(x, carry):
        for m in range(2):
            for group in range(groups):
                wide = queries[2 * x + m, :, group * width : (group + 1) * width]
                wide = wide.astype(jnp.float32)
                rows = [wide[:, at : at + HD] for at in range(0, width, HD)]
                o_ref[x * groups + group, m] = jnp.concatenate(rows, axis=0).astype(jnp.bfloat16)
        return carry

    lax.fori_loop(0, 4, one, 0)


def early_kernel(links_ref, place_ref, q_ref, own, eight, o_ref):
    per = q_ref.shape[2]
    step_sources = CHUNK // per
    for m in range(2):
        parts = [(own, m, None)]
        if m == 1:
            parts.append((own, 0, offset_of(links_ref, place_ref, 1, 0)))
        parts.append((eight, m, offset_of(links_ref, place_ref, m, 3)))

        def chunk(step, carry, m=m, parts=parts):
            start = step * step_sources
            query = q_ref[pl.ds(start, step_sources), m].reshape(CHUNK, HD)
            allowed = causal(start, CHUNK, per, place_ref[0], own.shape[2])
            total = weighted(query, None, parts, allowed)
            o_ref[pl.ds(start, step_sources), m] = total.reshape(step_sources, per, 2 * HD)
            return carry

        lax.fori_loop(0, q_ref.shape[0] // step_sources, chunk, 0)


def late_kernel(links_ref, place_ref, q_ref, early_ref, *refs):
    blocks = refs[:6]
    o_ref, k_all, v_all, s_all, peak, acc, bad_ref = refs[6:]
    own, one, two, eight, sixteen, thirtytwo = blocks
    zh = place_ref[0]
    keys = own.shape[2]
    per = q_ref.shape[2]
    bad_ref[...] = jnp.zeros_like(bad_ref)

    for m in range(2):
        step_sources = CHUNK // per
        sets = [(sixteen, m, 4), (thirtytwo, m, 5), (two, m, 2), (one, 1, m)]
        if m == 0:
            sets.append((one, 0, 1))
        parts = [
            (block, which, offset_of(links_ref, place_ref, m, slot)) for block, which, slot in sets
        ]

        def quick(step, carry, m=m, parts=parts):
            start = step * step_sources
            query = q_ref[pl.ds(start, step_sources), m].reshape(CHUNK, HD)
            total = early_ref[pl.ds(start, step_sources), m].reshape(CHUNK, 2 * HD)
            total = weighted(query, total, parts, None)
            summed = total[:, HD:]
            fine = (summed >= LEAST) & (summed <= MOST)
            result = (total[:, :HD] / summed).astype(jnp.bfloat16)
            o_ref[pl.ds(start, step_sources), m] = result.reshape(step_sources, per, HD)
            bad = jnp.where(fine, 0.0, 1.0)
            bad_ref[...] = jnp.maximum(bad_ref[...], jnp.max(bad.reshape(-1, 8, HD), axis=0))
            return carry

        lax.fori_loop(0, q_ref.shape[0] // step_sources, quick, 0)

    @pl.when(jnp.max(bad_ref[...]) > 0.0)
    def _():
        v_all[:, :, HD:] = jnp.ones((v_all.shape[0], keys, HD), jnp.bfloat16)
        for place, block in zip((OWN, ONE, TWO, EIGHT, SIXTEEN, THIRTYTWO), blocks):
            for m in range(2):
                k_all[place + m] = block[0, m]
                v_all[place + m, :, :HD] = block[1, m]
        step_sources = SAFE_CHUNK // per

        def sums_of(slot, index):
            top = peak[...]
            shifted = s_all[slot] - jnp.concatenate([top] * (keys // HD), axis=1)
            return jnp.dot(
                jnp.exp2(shifted).astype(jnp.bfloat16),
                v_all[index],
                preferred_element_type=jnp.float32,
            )

        def widest(scores):
            return functools.reduce(
                jnp.maximum, [scores[:, at : at + HD] for at in range(0, keys, HD)]
            )

        for m in range(2):

            def chunk(step, carry, m=m):
                start = step * step_sources
                query = q_ref[pl.ds(start, step_sources), m].reshape(SAFE_CHUNK, HD)
                allowed = causal(start, SAFE_CHUNK, per, zh, keys)
                scores = jnp.where(allowed, scores_of(query, k_all[OWN + m]), -1e30)
                s_all[0] = scores
                peak[...] = widest(scores)
                for slot, index in enumerate(SOURCES[m]):

                    @pl.when(live_of(links_ref, place_ref, m, slot))
                    def _(slot=slot, index=index):
                        scores = scores_of(query, k_all[index])
                        s_all[slot + 1] = scores
                        peak[...] = jnp.maximum(peak[...], widest(scores))

                top = jnp.max(peak[...], axis=1, keepdims=True)
                peak[...] = jnp.broadcast_to(top, (SAFE_CHUNK, HD))
                acc[...] = sums_of(0, OWN + m)
                for slot, index in enumerate(SOURCES[m]):

                    @pl.when(live_of(links_ref, place_ref, m, slot))
                    def _(slot=slot, index=index):
                        acc[...] += sums_of(slot + 1, index)

                result = (acc[:, :HD] / acc[:, HD:]).astype(jnp.bfloat16)
                o_ref[pl.ds(start, step_sources), m] = result.reshape(step_sources, per, HD)
                return carry

            lax.fori_loop(0, q_ref.shape[0] // step_sources, chunk, 0)


def call(kernel, outputs, scratch, flops, scalars, arrays):
    smem = pl.BlockSpec(memory_space=pltpu.SMEM)
    vmem = pl.BlockSpec(memory_space=pltpu.VMEM)
    return pl.pallas_call(
        kernel,
        out_shape=outputs,
        in_specs=[smem] * len(scalars) + [vmem] * len(arrays),
        out_specs=jax.tree.map(lambda _: vmem, outputs),
        scratch_shapes=scratch,
        compiler_params=pltpu.CompilerParams(vmem_limit_bytes=44 * 1024 * 1024),
        cost_estimate=pl.CostEstimate(flops=flops, bytes_accessed=2**20, transcendentals=0),
    )(*scalars, *arrays)


def pack_pairs(keys, values):
    resp, near, width = keys.shape
    output = jax.ShapeDtypeStruct((resp // 2 * width // HD, 2, 2, near, HD), jnp.bfloat16)
    block = pltpu.VMEM(keys.shape, keys.dtype)
    return pl.pallas_call(
        pack_pairs_kernel,
        out_shape=output,
        in_specs=[pl.BlockSpec(memory_space=pl.ANY)] * 2,
        out_specs=pl.BlockSpec(memory_space=pltpu.VMEM),
        scratch_shapes=[block, block, pltpu.SemaphoreType.DMA((2,))],
        compiler_params=pltpu.CompilerParams(vmem_limit_bytes=60 * 1024 * 1024),
    )(keys, values)


def join(mine, other):
    shape = mine.shape[:2] + (2 * mine.shape[2], HD)
    output = jax.ShapeDtypeStruct(shape, jnp.bfloat16)
    return call(join_kernel, output, [], 60 * 10**9, (), (mine, other))


def pack_queries(queries, groups):
    resp, near, width = queries.shape
    shape = (resp // 2 * groups, 2, near * width // groups // HD, HD)
    output = jax.ShapeDtypeStruct(shape, jnp.bfloat16)
    return call(pack_queries_kernel, output, [], 10**6, (), (queries,))


def attend_early(links, place, query, *blocks):
    output = jax.ShapeDtypeStruct(query.shape[:3] + (2 * HD,), jnp.float32)
    return call(early_kernel, output, [], 4 * 10**9, (links, place), (query,) + blocks)


def attend_late(links, place, query, early, *blocks):
    keys = blocks[0].shape[2]
    output = jax.ShapeDtypeStruct(query.shape, jnp.bfloat16)
    scratch = [
        pltpu.VMEM((12, keys, HD), jnp.bfloat16),
        pltpu.VMEM((12, keys, 2 * HD), jnp.bfloat16),
        pltpu.VMEM((SLOTS + 1, SAFE_CHUNK, keys), jnp.float32),
        pltpu.VMEM((SAFE_CHUNK, HD), jnp.float32),
        pltpu.VMEM((SAFE_CHUNK, 2 * HD), jnp.float32),
        pltpu.VMEM((8, HD), jnp.float32),
    ]
    return call(late_kernel, output, scratch, 6 * 10**9, (links, place), (query, early) + blocks)


def ring(value, by, keep=lambda h: True):
    pairs = [(z, (z + by) % 16) for z in range(16) if keep(z % 8)]
    return lax.ppermute(value, ("zh", "h"), pairs)


def along(value, by):
    return ring(value, by, lambda h: h + by < 8)


def across(value, by):
    return lax.ppermute(value, "x", [(x, (x + by) % 4) for x in range(4)])


def local(queries, keys, values, links):
    resp, near, width = queries.shape
    groups = keys.shape[2] // HD
    repeat = width // keys.shape[2]
    x, zh, h = lax.axis_index("x"), lax.axis_index("zh"), lax.axis_index("h")

    with jax.named_scope("key_value_exchange"):
        own = pack_pairs(keys, values)
        own = lax.all_to_all(own, PLANE, split_axis=0, concat_axis=0, tiled=True)
        own = own.transpose(1, 2, 0, 3, 4).reshape(2, 2, 4 * groups * near, HD)
        own = join(own, ring(own, 8))
    with jax.named_scope("query_exchange"):
        query = pack_queries(queries, groups)
        query = lax.all_to_all(query, PLANE, split_axis=0, concat_axis=0, tiled=True)
    place = jnp.stack([zh, h * resp + 2 * x]).astype(jnp.int32)
    with jax.named_scope("key_value_spread"):
        eight = along(own, 1)
        thirtytwo = ring(own, -4, lambda h: h < 4)
        sixteen = along(own, 2)
        two = across(jnp.where(x >= 2, eight, own), 2)
        one = across(jnp.where(x >= 3, eight, own), 1)
    with jax.named_scope("attend"):
        links = links.T
        early = attend_early(links, place, query, own, eight)
        result = attend_late(links, place, query, early, own, one, two, eight, sixteen, thirtytwo)
    with jax.named_scope("return_exchange"):
        result = lax.all_to_all(result, PLANE, split_axis=0, concat_axis=0, tiled=True)
        result = result.reshape(4, groups, 2, repeat, near, HD).transpose(0, 2, 4, 1, 3, 5)
        return result.reshape(resp, near, width)


def solution(mesh):
    fine = Mesh(mesh.devices.reshape(4, 2, 4, 2, 8), ("x", "zh", "y", "c", "h"))
    placed = P("h", ("x", "zh", "y", "c"), None)
    return jax.shard_map(
        local, mesh=fine, in_specs=(placed, placed, placed, P()), out_specs=placed, check_vma=False
    )
```

```python
import functools
import math

import jax
import jax.numpy as jnp
from jax import lax
from jax.experimental import pallas as pl
from jax.experimental.pallas import tpu as pltpu
from jax.sharding import Mesh, PartitionSpec as P

HD = 128
SLOTS = 6
FACTOR = HD ** (-0.5) * math.log2(math.e)
CHUNK = 2048
SAFE_CHUNK = 512
LEAST, MOST = 2.0**-60, 2.0**60
PLANE = ("x", "y", "c")
OWN, ONE, TWO, EIGHT, SIXTEEN, THIRTYTWO = 0, 2, 4, 6, 8, 10
SOURCES = (
    (ONE + 1, ONE, TWO, EIGHT, SIXTEEN, THIRTYTWO),
    (OWN, ONE + 1, TWO + 1, EIGHT + 1, SIXTEEN + 1, THIRTYTWO + 1),
)


def scores_of(query, key_block):
    dims = (((1,), (1,)), ((), ()))
    return lax.dot_general(query, key_block, dims, preferred_element_type=jnp.float32) * FACTOR


def causal(start, count, per, zh, keys):
    key = lax.broadcasted_iota(jnp.int32, (1, keys), 1)
    inner = key % (keys // 2)
    key_half = jnp.where(key < keys // 2, zh, 1 - zh)
    key_pos = (inner // 32) * 64 + key_half * 32 + inner % 32
    row = lax.broadcasted_iota(jnp.int32, (count, 1), 0)
    source = start + row // per
    query_pos = (source // 8) * 64 + zh * 32 + (source % 8) * 4 + row % 4
    return key_pos <= query_pos


def weighted(query, total, parts, allowed):
    weights, values = [], []
    for at, (block, which, offset) in enumerate(parts):
        scores = scores_of(query, block[0, which])
        weight = jnp.exp2(scores if offset is None else scores + offset)
        if allowed is not None and at == 0:
            weight = jnp.where(allowed, weight, 0.0)
        weights.append(weight.astype(jnp.bfloat16))
        value_block = block[1, which]
        values.append(jnp.concatenate([value_block, jnp.ones_like(value_block)], axis=1))
    term = jnp.dot(
        jnp.concatenate(weights, axis=1),
        jnp.concatenate(values, axis=0),
        preferred_element_type=jnp.float32,
    )
    return term if total is None else total + term


def live_of(links_ref, place_ref, m, slot):
    index = place_ref[1] + m
    return links_ref[slot, index] != index


def offset_of(links_ref, place_ref, m, slot):
    return jnp.where(live_of(links_ref, place_ref, m, slot), 0.0, -1e30)


def pack_pairs_kernel(keys, values, o_ref):
    groups = keys.shape[2] // HD
    for x in range(4):
        for group in range(groups):
            columns = slice(group * HD, (group + 1) * HD)
            for kind, array in enumerate((keys, values)):
                for m in range(2):
                    piece = array[2 * x + m, :, columns]
                    o_ref[x * groups + group, kind, m] = piece


def join_kernel(mine, other, o_ref):
    half_keys = mine.shape[2]
    o_ref[:, :, :half_keys] = mine[...]
    o_ref[:, :, half_keys:] = other[...]


def pack_queries_kernel(queries, o_ref):
    groups = o_ref.shape[0] // 4
    width = queries.shape[2] // groups

    def one(x, carry):
        for m in range(2):
            for group in range(groups):
                wide = queries[2 * x + m, :, group * width : (group + 1) * width]
                wide = wide.astype(jnp.float32)
                rows = [wide[:, at : at + HD] for at in range(0, width, HD)]
                o_ref[x * groups + group, m] = jnp.concatenate(rows, axis=0).astype(jnp.bfloat16)
        return carry

    lax.fori_loop(0, 4, one, 0)


def early_kernel(links_ref, place_ref, q_ref, own, eight, o_ref):
    per = q_ref.shape[2]
    step_sources = CHUNK // per
    for m in range(2):
        parts = [(own, m, None)]
        if m == 1:
            parts.append((own, 0, offset_of(links_ref, place_ref, 1, 0)))
        parts.append((eight, m, offset_of(links_ref, place_ref, m, 3)))

        def chunk(step, carry, m=m, parts=parts):
            start = step * step_sources
            query = q_ref[pl.ds(start, step_sources), m].reshape(CHUNK, HD)
            allowed = causal(start, CHUNK, per, place_ref[0], own.shape[2])
            total = weighted(query, None, parts, allowed)
            o_ref[pl.ds(start, step_sources), m] = total.reshape(step_sources, per, 2 * HD)
            return carry

        lax.fori_loop(0, q_ref.shape[0] // step_sources, chunk, 0)


def late_kernel(links_ref, place_ref, q_ref, early_ref, *refs):
    blocks = refs[:6]
    o_ref, k_all, v_all, s_all, peak, acc, bad_ref = refs[6:]
    own, one, two, eight, sixteen, thirtytwo = blocks
    zh = place_ref[0]
    keys = own.shape[2]
    per = q_ref.shape[2]
    bad_ref[...] = jnp.zeros_like(bad_ref)

    for m in range(2):
        step_sources = CHUNK // per
        sets = [(sixteen, m, 4), (thirtytwo, m, 5), (two, m, 2), (one, 1, m)]
        if m == 0:
            sets.append((one, 0, 1))
        parts = [
            (block, which, offset_of(links_ref, place_ref, m, slot)) for block, which, slot in sets
        ]

        def quick(step, carry, m=m, parts=parts):
            start = step * step_sources
            query = q_ref[pl.ds(start, step_sources), m].reshape(CHUNK, HD)
            total = early_ref[pl.ds(start, step_sources), m].reshape(CHUNK, 2 * HD)
            total = weighted(query, total, parts, None)
            summed = total[:, HD:]
            fine = (summed >= LEAST) & (summed <= MOST)
            result = (total[:, :HD] / summed).astype(jnp.bfloat16)
            o_ref[pl.ds(start, step_sources), m] = result.reshape(step_sources, per, HD)
            bad = jnp.where(fine, 0.0, 1.0)
            bad_ref[...] = jnp.maximum(bad_ref[...], jnp.max(bad.reshape(-1, 8, HD), axis=0))
            return carry

        lax.fori_loop(0, q_ref.shape[0] // step_sources, quick, 0)

    @pl.when(jnp.max(bad_ref[...]) > 0.0)
    def _():
        v_all[:, :, HD:] = jnp.ones((v_all.shape[0], keys, HD), jnp.bfloat16)
        for place, block in zip((OWN, ONE, TWO, EIGHT, SIXTEEN, THIRTYTWO), blocks):
            for m in range(2):
                k_all[place + m] = block[0, m]
                v_all[place + m, :, :HD] = block[1, m]
        step_sources = SAFE_CHUNK // per

        def sums_of(slot, index):
            top = peak[...]
            shifted = s_all[slot] - jnp.concatenate([top] * (keys // HD), axis=1)
            return jnp.dot(
                jnp.exp2(shifted).astype(jnp.bfloat16),
                v_all[index],
                preferred_element_type=jnp.float32,
            )

        def widest(scores):
            return functools.reduce(
                jnp.maximum, [scores[:, at : at + HD] for at in range(0, keys, HD)]
            )

        for m in range(2):

            def chunk(step, carry, m=m):
                start = step * step_sources
                query = q_ref[pl.ds(start, step_sources), m].reshape(SAFE_CHUNK, HD)
                allowed = causal(start, SAFE_CHUNK, per, zh, keys)
                scores = jnp.where(allowed, scores_of(query, k_all[OWN + m]), -1e30)
                s_all[0] = scores
                peak[...] = widest(scores)
                for slot, index in enumerate(SOURCES[m]):

                    @pl.when(live_of(links_ref, place_ref, m, slot))
                    def _(slot=slot, index=index):
                        scores = scores_of(query, k_all[index])
                        s_all[slot + 1] = scores
                        peak[...] = jnp.maximum(peak[...], widest(scores))

                top = jnp.max(peak[...], axis=1, keepdims=True)
                peak[...] = jnp.broadcast_to(top, (SAFE_CHUNK, HD))
                acc[...] = sums_of(0, OWN + m)
                for slot, index in enumerate(SOURCES[m]):

                    @pl.when(live_of(links_ref, place_ref, m, slot))
                    def _(slot=slot, index=index):
                        acc[...] += sums_of(slot + 1, index)

                result = (acc[:, :HD] / acc[:, HD:]).astype(jnp.bfloat16)
                o_ref[pl.ds(start, step_sources), m] = result.reshape(step_sources, per, HD)
                return carry

            lax.fori_loop(0, q_ref.shape[0] // step_sources, chunk, 0)


def call(kernel, outputs, scratch, flops, scalars, arrays):
    smem = pl.BlockSpec(memory_space=pltpu.SMEM)
    vmem = pl.BlockSpec(memory_space=pltpu.VMEM)
    return pl.pallas_call(
        kernel,
        out_shape=outputs,
        in_specs=[smem] * len(scalars) + [vmem] * len(arrays),
        out_specs=jax.tree.map(lambda _: vmem, outputs),
        scratch_shapes=scratch,
        compiler_params=pltpu.CompilerParams(vmem_limit_bytes=44 * 1024 * 1024),
        cost_estimate=pl.CostEstimate(flops=flops, bytes_accessed=2**20, transcendentals=0),
    )(*scalars, *arrays)


def pack_pairs(keys, values):
    resp, near, width = keys.shape
    output = jax.ShapeDtypeStruct((resp // 2 * width // HD, 2, 2, near, HD), jnp.bfloat16)
    return pl.pallas_call(
        pack_pairs_kernel,
        out_shape=output,
        in_specs=[pl.BlockSpec(memory_space=pltpu.VMEM)] * 2,
        out_specs=pl.BlockSpec(memory_space=pltpu.VMEM),
        compiler_params=pltpu.CompilerParams(vmem_limit_bytes=60 * 1024 * 1024),
    )(keys, values)


def join(mine, other):
    shape = mine.shape[:2] + (2 * mine.shape[2], HD)
    output = jax.ShapeDtypeStruct(shape, jnp.bfloat16)
    return call(join_kernel, output, [], 60 * 10**9, (), (mine, other))


def pack_queries(queries, groups):
    resp, near, width = queries.shape
    shape = (resp // 2 * groups, 2, near * width // groups // HD, HD)
    output = jax.ShapeDtypeStruct(shape, jnp.bfloat16)
    return call(pack_queries_kernel, output, [], 10**6, (), (queries,))


def attend_early(links, place, query, *blocks):
    output = jax.ShapeDtypeStruct(query.shape[:3] + (2 * HD,), jnp.float32)
    return call(early_kernel, output, [], 4 * 10**9, (links, place), (query,) + blocks)


def attend_late(links, place, query, early, *blocks):
    keys = blocks[0].shape[2]
    output = jax.ShapeDtypeStruct(query.shape, jnp.bfloat16)
    scratch = [
        pltpu.VMEM((12, keys, HD), jnp.bfloat16),
        pltpu.VMEM((12, keys, 2 * HD), jnp.bfloat16),
        pltpu.VMEM((SLOTS + 1, SAFE_CHUNK, keys), jnp.float32),
        pltpu.VMEM((SAFE_CHUNK, HD), jnp.float32),
        pltpu.VMEM((SAFE_CHUNK, 2 * HD), jnp.float32),
        pltpu.VMEM((8, HD), jnp.float32),
    ]
    return call(late_kernel, output, scratch, 6 * 10**9, (links, place), (query, early) + blocks)


def ring(value, by, keep=lambda h: True):
    pairs = [(z, (z + by) % 16) for z in range(16) if keep(z % 8)]
    return lax.ppermute(value, ("zh", "h"), pairs)


def along(value, by):
    return ring(value, by, lambda h: h + by < 8)


def across(value, by):
    return lax.ppermute(value, "x", [(x, (x + by) % 4) for x in range(4)])


def local(queries, keys, values, links):
    resp, near, width = queries.shape
    groups = keys.shape[2] // HD
    repeat = width // keys.shape[2]
    x, zh, h = lax.axis_index("x"), lax.axis_index("zh"), lax.axis_index("h")

    with jax.named_scope("key_value_exchange"):
        own = pack_pairs(keys, values)
        own = lax.all_to_all(own, PLANE, split_axis=0, concat_axis=0, tiled=True)
        own = own.transpose(1, 2, 0, 3, 4).reshape(2, 2, 4 * groups * near, HD)
        own = join(own, ring(own, 8))
    with jax.named_scope("query_exchange"):
        query = pack_queries(queries, groups)
        query = lax.all_to_all(query, PLANE, split_axis=0, concat_axis=0, tiled=True)
    place = jnp.stack([zh, h * resp + 2 * x]).astype(jnp.int32)
    with jax.named_scope("key_value_spread"):
        eight = along(own, 1)
        thirtytwo = ring(own, -4, lambda h: h < 4)
        sixteen = along(own, 2)
        two = across(jnp.where(x >= 2, eight, own), 2)
        one = across(jnp.where(x >= 3, eight, own), 1)
    with jax.named_scope("attend"):
        links = links.T
        early = attend_early(links, place, query, own, eight)
        result = attend_late(links, place, query, early, own, one, two, eight, sixteen, thirtytwo)
    with jax.named_scope("return_exchange"):
        result = lax.all_to_all(result, PLANE, split_axis=0, concat_axis=0, tiled=True)
        result = result.reshape(4, groups, 2, repeat, near, HD).transpose(0, 2, 4, 1, 3, 5)
        return result.reshape(resp, near, width)


def solution(mesh):
    fine = Mesh(mesh.devices.reshape(4, 2, 4, 2, 8), ("x", "zh", "y", "c", "h"))
    placed = P("h", ("x", "zh", "y", "c"), None)
    return jax.shard_map(
        local, mesh=fine, in_specs=(placed, placed, placed, P()), out_specs=placed, check_vma=False
    )
```

```python
import functools
import math

import jax
import jax.numpy as jnp
from jax import lax
from jax.experimental import pallas as pl
from jax.experimental.pallas import tpu as pltpu
from jax.sharding import Mesh, PartitionSpec as P

HD = 128
SLOTS = 6
FACTOR = HD ** (-0.5) * math.log2(math.e)
CHUNK = 2048
SAFE_CHUNK = 512
LEAST, MOST = 2.0**-60, 2.0**60
PLANE = ("x", "y", "c")
OWN, ONE, TWO, EIGHT, SIXTEEN, THIRTYTWO = 0, 2, 4, 6, 8, 10
SOURCES = (
    (ONE + 1, ONE, TWO, EIGHT, SIXTEEN, THIRTYTWO),
    (OWN, ONE + 1, TWO + 1, EIGHT + 1, SIXTEEN + 1, THIRTYTWO + 1),
)


def scores_of(query, key_block):
    dims = (((1,), (1,)), ((), ()))
    return lax.dot_general(query, key_block, dims, preferred_element_type=jnp.float32) * FACTOR


def causal(start, count, per, zh, keys):
    key = lax.broadcasted_iota(jnp.int32, (1, keys), 1)
    inner = key % (keys // 2)
    key_half = jnp.where(key < keys // 2, zh, 1 - zh)
    key_pos = (inner // 32) * 64 + key_half * 32 + inner % 32
    row = lax.broadcasted_iota(jnp.int32, (count, 1), 0)
    source = start + row // per
    query_pos = (source // 8) * 64 + zh * 32 + (source % 8) * 4 + row % 4
    return key_pos <= query_pos


def weighted(query, total, parts, allowed):
    weights, values = [], []
    for at, (block, which, offset) in enumerate(parts):
        scores = scores_of(query, block[0, which])
        weight = jnp.exp2(scores if offset is None else scores + offset)
        if allowed is not None and at == 0:
            weight = jnp.where(allowed, weight, 0.0)
        weights.append(weight.astype(jnp.bfloat16))
        value_block = block[1, which]
        values.append(jnp.concatenate([value_block, jnp.ones_like(value_block)], axis=1))
    term = jnp.dot(
        jnp.concatenate(weights, axis=1),
        jnp.concatenate(values, axis=0),
        preferred_element_type=jnp.float32,
    )
    return term if total is None else total + term


def live_of(links_ref, place_ref, m, slot):
    index = place_ref[1] + m
    return links_ref[slot, index] != index


def offset_of(links_ref, place_ref, m, slot):
    return jnp.where(live_of(links_ref, place_ref, m, slot), 0.0, -1e30)


def pack_pairs_kernel(keys, values, o_ref):
    groups = keys.shape[2] // HD
    for x in range(4):
        for group in range(groups):
            columns = slice(group * HD, (group + 1) * HD)
            for kind, array in enumerate((keys, values)):
                for m in range(2):
                    piece = array[2 * x + m, :, columns]
                    o_ref[x * groups + group, kind, m] = piece


def join_kernel(mine, other, o_ref):
    half_keys = mine.shape[2]
    o_ref[:, :, :half_keys] = mine[...]
    o_ref[:, :, half_keys:] = other[...]


def pack_queries_kernel(queries, o_ref):
    groups = o_ref.shape[0] // 4
    width = queries.shape[2] // groups

    def one(x, carry):
        for m in range(2):
            for group in range(groups):
                wide = queries[2 * x + m, :, group * width : (group + 1) * width]
                wide = wide.astype(jnp.float32)
                rows = [wide[:, at : at + HD] for at in range(0, width, HD)]
                o_ref[x * groups + group, m] = jnp.concatenate(rows, axis=0).astype(jnp.bfloat16)
        return carry

    lax.fori_loop(0, 4, one, 0)


def early_kernel(links_ref, place_ref, q_ref, own, eight, sixteen, o_ref):
    per = q_ref.shape[2]
    step_sources = CHUNK // per
    for m in range(2):
        parts = [(own, m, None)]
        if m == 1:
            parts.append((own, 0, offset_of(links_ref, place_ref, 1, 0)))
        parts.append((eight, m, offset_of(links_ref, place_ref, m, 3)))
        parts.append((sixteen, m, offset_of(links_ref, place_ref, m, 4)))

        def chunk(step, carry, m=m, parts=parts):
            start = step * step_sources
            query = q_ref[pl.ds(start, step_sources), m].reshape(CHUNK, HD)
            allowed = causal(start, CHUNK, per, place_ref[0], own.shape[2])
            total = weighted(query, None, parts, allowed)
            o_ref[pl.ds(start, step_sources), m] = total.reshape(step_sources, per, 2 * HD)
            return carry

        lax.fori_loop(0, q_ref.shape[0] // step_sources, chunk, 0)


def late_kernel(links_ref, place_ref, q_ref, early_ref, *refs):
    blocks = refs[:6]
    o_ref, k_all, v_all, s_all, peak, acc, bad_ref = refs[6:]
    own, one, two, eight, sixteen, thirtytwo = blocks
    zh = place_ref[0]
    keys = own.shape[2]
    per = q_ref.shape[2]
    bad_ref[...] = jnp.zeros_like(bad_ref)

    for m in range(2):
        step_sources = CHUNK // per
        sets = [(thirtytwo, m, 5), (two, m, 2), (one, 1, m)]
        if m == 0:
            sets.append((one, 0, 1))
        parts = [
            (block, which, offset_of(links_ref, place_ref, m, slot)) for block, which, slot in sets
        ]

        def quick(step, carry, m=m, parts=parts):
            start = step * step_sources
            query = q_ref[pl.ds(start, step_sources), m].reshape(CHUNK, HD)
            total = early_ref[pl.ds(start, step_sources), m].reshape(CHUNK, 2 * HD)
            total = weighted(query, total, parts, None)
            summed = total[:, HD:]
            fine = (summed >= LEAST) & (summed <= MOST)
            result = (total[:, :HD] / summed).astype(jnp.bfloat16)
            o_ref[pl.ds(start, step_sources), m] = result.reshape(step_sources, per, HD)
            bad = jnp.where(fine, 0.0, 1.0)
            bad_ref[...] = jnp.maximum(bad_ref[...], jnp.max(bad.reshape(-1, 8, HD), axis=0))
            return carry

        lax.fori_loop(0, q_ref.shape[0] // step_sources, quick, 0)

    @pl.when(jnp.max(bad_ref[...]) > 0.0)
    def _():
        v_all[:, :, HD:] = jnp.ones((v_all.shape[0], keys, HD), jnp.bfloat16)
        for place, block in zip((OWN, ONE, TWO, EIGHT, SIXTEEN, THIRTYTWO), blocks):
            for m in range(2):
                k_all[place + m] = block[0, m]
                v_all[place + m, :, :HD] = block[1, m]
        step_sources = SAFE_CHUNK // per

        def sums_of(slot, index):
            top = peak[...]
            shifted = s_all[slot] - jnp.concatenate([top] * (keys // HD), axis=1)
            return jnp.dot(
                jnp.exp2(shifted).astype(jnp.bfloat16),
                v_all[index],
                preferred_element_type=jnp.float32,
            )

        def widest(scores):
            return functools.reduce(
                jnp.maximum, [scores[:, at : at + HD] for at in range(0, keys, HD)]
            )

        for m in range(2):

            def chunk(step, carry, m=m):
                start = step * step_sources
                query = q_ref[pl.ds(start, step_sources), m].reshape(SAFE_CHUNK, HD)
                allowed = causal(start, SAFE_CHUNK, per, zh, keys)
                scores = jnp.where(allowed, scores_of(query, k_all[OWN + m]), -1e30)
                s_all[0] = scores
                peak[...] = widest(scores)
                for slot, index in enumerate(SOURCES[m]):

                    @pl.when(live_of(links_ref, place_ref, m, slot))
                    def _(slot=slot, index=index):
                        scores = scores_of(query, k_all[index])
                        s_all[slot + 1] = scores
                        peak[...] = jnp.maximum(peak[...], widest(scores))

                top = jnp.max(peak[...], axis=1, keepdims=True)
                peak[...] = jnp.broadcast_to(top, (SAFE_CHUNK, HD))
                acc[...] = sums_of(0, OWN + m)
                for slot, index in enumerate(SOURCES[m]):

                    @pl.when(live_of(links_ref, place_ref, m, slot))
                    def _(slot=slot, index=index):
                        acc[...] += sums_of(slot + 1, index)

                result = (acc[:, :HD] / acc[:, HD:]).astype(jnp.bfloat16)
                o_ref[pl.ds(start, step_sources), m] = result.reshape(step_sources, per, HD)
                return carry

            lax.fori_loop(0, q_ref.shape[0] // step_sources, chunk, 0)


def call(kernel, outputs, scratch, flops, scalars, arrays):
    smem = pl.BlockSpec(memory_space=pltpu.SMEM)
    vmem = pl.BlockSpec(memory_space=pltpu.VMEM)
    return pl.pallas_call(
        kernel,
        out_shape=outputs,
        in_specs=[smem] * len(scalars) + [vmem] * len(arrays),
        out_specs=jax.tree.map(lambda _: vmem, outputs),
        scratch_shapes=scratch,
        compiler_params=pltpu.CompilerParams(vmem_limit_bytes=44 * 1024 * 1024),
        cost_estimate=pl.CostEstimate(flops=flops, bytes_accessed=2**20, transcendentals=0),
    )(*scalars, *arrays)


def pack_pairs(keys, values):
    resp, near, width = keys.shape
    output = jax.ShapeDtypeStruct((resp // 2 * width // HD, 2, 2, near, HD), jnp.bfloat16)
    return pl.pallas_call(
        pack_pairs_kernel,
        out_shape=output,
        in_specs=[pl.BlockSpec(memory_space=pltpu.VMEM)] * 2,
        out_specs=pl.BlockSpec(memory_space=pltpu.VMEM),
        compiler_params=pltpu.CompilerParams(vmem_limit_bytes=60 * 1024 * 1024),
    )(keys, values)


def join(mine, other):
    shape = mine.shape[:2] + (2 * mine.shape[2], HD)
    output = jax.ShapeDtypeStruct(shape, jnp.bfloat16)
    return call(join_kernel, output, [], 60 * 10**9, (), (mine, other))


def pack_queries(queries, groups):
    resp, near, width = queries.shape
    shape = (resp // 2 * groups, 2, near * width // groups // HD, HD)
    output = jax.ShapeDtypeStruct(shape, jnp.bfloat16)
    return call(pack_queries_kernel, output, [], 10**6, (), (queries,))


def attend_early(links, place, query, *blocks):
    output = jax.ShapeDtypeStruct(query.shape[:3] + (2 * HD,), jnp.float32)
    return call(early_kernel, output, [], 4 * 10**9, (links, place), (query,) + blocks)


def attend_late(links, place, query, early, *blocks):
    keys = blocks[0].shape[2]
    output = jax.ShapeDtypeStruct(query.shape, jnp.bfloat16)
    scratch = [
        pltpu.VMEM((12, keys, HD), jnp.bfloat16),
        pltpu.VMEM((12, keys, 2 * HD), jnp.bfloat16),
        pltpu.VMEM((SLOTS + 1, SAFE_CHUNK, keys), jnp.float32),
        pltpu.VMEM((SAFE_CHUNK, HD), jnp.float32),
        pltpu.VMEM((SAFE_CHUNK, 2 * HD), jnp.float32),
        pltpu.VMEM((8, HD), jnp.float32),
    ]
    return call(late_kernel, output, scratch, 6 * 10**9, (links, place), (query, early) + blocks)


def ring(value, by, keep=lambda h: True):
    pairs = [(z, (z + by) % 16) for z in range(16) if keep(z % 8)]
    return lax.ppermute(value, ("zh", "h"), pairs)


def along(value, by):
    return ring(value, by, lambda h: h + by < 8)


def across(value, by):
    return lax.ppermute(value, "x", [(x, (x + by) % 4) for x in range(4)])


def local(queries, keys, values, links):
    resp, near, width = queries.shape
    groups = keys.shape[2] // HD
    repeat = width // keys.shape[2]
    x, zh, h = lax.axis_index("x"), lax.axis_index("zh"), lax.axis_index("h")

    with jax.named_scope("key_value_exchange"):
        own = pack_pairs(keys, values)
        own = lax.all_to_all(own, PLANE, split_axis=0, concat_axis=0, tiled=True)
        own = own.transpose(1, 2, 0, 3, 4).reshape(2, 2, 4 * groups * near, HD)
        own = join(own, ring(own, 8))
    with jax.named_scope("query_exchange"):
        query = pack_queries(queries, groups)
        query = lax.all_to_all(query, PLANE, split_axis=0, concat_axis=0, tiled=True)
    place = jnp.stack([zh, h * resp + 2 * x]).astype(jnp.int32)
    with jax.named_scope("key_value_spread"):
        eight = along(own, 1)
        thirtytwo = ring(own, -4, lambda h: h < 4)
        sixteen = along(own, 2)
        two = across(jnp.where(x >= 2, eight, own), 2)
        one = across(jnp.where(x >= 3, eight, own), 1)
    with jax.named_scope("attend"):
        links = links.T
        early = attend_early(links, place, query, own, eight, sixteen)
        result = attend_late(links, place, query, early, own, one, two, eight, sixteen, thirtytwo)
    with jax.named_scope("return_exchange"):
        result = lax.all_to_all(result, PLANE, split_axis=0, concat_axis=0, tiled=True)
        result = result.reshape(4, groups, 2, repeat, near, HD).transpose(0, 2, 4, 1, 3, 5)
        return result.reshape(resp, near, width)


def solution(mesh):
    fine = Mesh(mesh.devices.reshape(4, 2, 4, 2, 8), ("x", "zh", "y", "c", "h"))
    placed = P("h", ("x", "zh", "y", "c"), None)
    return jax.shard_map(
        local, mesh=fine, in_specs=(placed, placed, placed, P()), out_specs=placed, check_vma=False
    )
```

```python
import functools
import math

import jax
import jax.numpy as jnp
from jax import lax
from jax.experimental import pallas as pl
from jax.experimental.pallas import tpu as pltpu
from jax.sharding import Mesh, PartitionSpec as P

HD = 128
SLOTS = 6
FACTOR = HD ** (-0.5) * math.log2(math.e)
CHUNK = 2048
EARLY_CHUNK = 1024
SAFE_CHUNK = 512
LEAST, MOST = 2.0**-60, 2.0**60
PLANE = ("x", "y", "c")
OWN, ONE, TWO, EIGHT, SIXTEEN, THIRTYTWO = 0, 2, 4, 6, 8, 10
SOURCES = (
    (ONE + 1, ONE, TWO, EIGHT, SIXTEEN, THIRTYTWO),
    (OWN, ONE + 1, TWO + 1, EIGHT + 1, SIXTEEN + 1, THIRTYTWO + 1),
)


def scores_of(query, key_block):
    dims = (((1,), (1,)), ((), ()))
    return lax.dot_general(query, key_block, dims, preferred_element_type=jnp.float32) * FACTOR


def causal(start, count, per, zh, keys):
    key = lax.broadcasted_iota(jnp.int32, (1, keys), 1)
    inner = key % (keys // 2)
    key_half = jnp.where(key < keys // 2, zh, 1 - zh)
    key_pos = (inner // 32) * 64 + key_half * 32 + inner % 32
    row = lax.broadcasted_iota(jnp.int32, (count, 1), 0)
    source = start + row // per
    query_pos = (source // 8) * 64 + zh * 32 + (source % 8) * 4 + row % 4
    return key_pos <= query_pos


def weighted(query, total, parts, allowed):
    weights, values = [], []
    for at, (block, which, offset) in enumerate(parts):
        scores = scores_of(query, block[0, which])
        weight = jnp.exp2(scores if offset is None else scores + offset)
        if allowed is not None and at == 0:
            weight = jnp.where(allowed, weight, 0.0)
        weights.append(weight.astype(jnp.bfloat16))
        value_block = block[1, which]
        values.append(jnp.concatenate([value_block, jnp.ones_like(value_block)], axis=1))
    term = jnp.dot(
        jnp.concatenate(weights, axis=1),
        jnp.concatenate(values, axis=0),
        preferred_element_type=jnp.float32,
    )
    return term if total is None else total + term


def live_of(links_ref, place_ref, m, slot):
    index = place_ref[1] + m
    return links_ref[slot, index] != index


def offset_of(links_ref, place_ref, m, slot):
    return jnp.where(live_of(links_ref, place_ref, m, slot), 0.0, -1e30)


def pack_pairs_kernel(keys, values, o_ref):
    groups = keys.shape[2] // HD
    for x in range(4):
        for group in range(groups):
            columns = slice(group * HD, (group + 1) * HD)
            for kind, array in enumerate((keys, values)):
                for m in range(2):
                    piece = array[2 * x + m, :, columns]
                    o_ref[x * groups + group, kind, m] = piece


def join_kernel(mine, other, o_ref):
    half_keys = mine.shape[2]
    o_ref[:, :, :half_keys] = mine[...]
    o_ref[:, :, half_keys:] = other[...]


def pack_queries_kernel(queries, o_ref):
    groups = o_ref.shape[0] // 4
    width = queries.shape[2] // groups

    def one(x, carry):
        for m in range(2):
            for group in range(groups):
                wide = queries[2 * x + m, :, group * width : (group + 1) * width]
                wide = wide.astype(jnp.float32)
                rows = [wide[:, at : at + HD] for at in range(0, width, HD)]
                o_ref[x * groups + group, m] = jnp.concatenate(rows, axis=0).astype(jnp.bfloat16)
        return carry

    lax.fori_loop(0, 4, one, 0)


def early_kernel(links_ref, place_ref, q_ref, own, eight, o_ref):
    per = q_ref.shape[2]
    step_sources = EARLY_CHUNK // per
    for m in range(2):
        parts = [(own, m, None)]
        if m == 1:
            parts.append((own, 0, offset_of(links_ref, place_ref, 1, 0)))
        parts.append((eight, m, offset_of(links_ref, place_ref, m, 3)))

        def chunk(step, carry, m=m, parts=parts):
            start = step * step_sources
            query = q_ref[pl.ds(start, step_sources), m].reshape(EARLY_CHUNK, HD)
            allowed = causal(start, EARLY_CHUNK, per, place_ref[0], own.shape[2])
            total = weighted(query, None, parts, allowed)
            o_ref[pl.ds(start, step_sources), m] = total.reshape(step_sources, per, 2 * HD)
            return carry

        lax.fori_loop(0, q_ref.shape[0] // step_sources, chunk, 0)


def late_kernel(links_ref, place_ref, q_ref, early_ref, *refs):
    blocks = refs[:6]
    o_ref, k_all, v_all, s_all, peak, acc, bad_ref = refs[6:]
    own, one, two, eight, sixteen, thirtytwo = blocks
    zh = place_ref[0]
    keys = own.shape[2]
    per = q_ref.shape[2]
    bad_ref[...] = jnp.zeros_like(bad_ref)

    for m in range(2):
        step_sources = CHUNK // per
        sets = [(sixteen, m, 4), (thirtytwo, m, 5), (two, m, 2), (one, 1, m)]
        if m == 0:
            sets.append((one, 0, 1))
        parts = [
            (block, which, offset_of(links_ref, place_ref, m, slot)) for block, which, slot in sets
        ]

        def quick(step, carry, m=m, parts=parts):
            start = step * step_sources
            query = q_ref[pl.ds(start, step_sources), m].reshape(CHUNK, HD)
            total = early_ref[pl.ds(start, step_sources), m].reshape(CHUNK, 2 * HD)
            total = weighted(query, total, parts, None)
            summed = total[:, HD:]
            fine = (summed >= LEAST) & (summed <= MOST)
            result = (total[:, :HD] / summed).astype(jnp.bfloat16)
            o_ref[pl.ds(start, step_sources), m] = result.reshape(step_sources, per, HD)
            bad = jnp.where(fine, 0.0, 1.0)
            bad_ref[...] = jnp.maximum(bad_ref[...], jnp.max(bad.reshape(-1, 8, HD), axis=0))
            return carry

        lax.fori_loop(0, q_ref.shape[0] // step_sources, quick, 0)

    @pl.when(jnp.max(bad_ref[...]) > 0.0)
    def _():
        v_all[:, :, HD:] = jnp.ones((v_all.shape[0], keys, HD), jnp.bfloat16)
        for place, block in zip((OWN, ONE, TWO, EIGHT, SIXTEEN, THIRTYTWO), blocks):
            for m in range(2):
                k_all[place + m] = block[0, m]
                v_all[place + m, :, :HD] = block[1, m]
        step_sources = SAFE_CHUNK // per

        def sums_of(slot, index):
            top = peak[...]
            shifted = s_all[slot] - jnp.concatenate([top] * (keys // HD), axis=1)
            return jnp.dot(
                jnp.exp2(shifted).astype(jnp.bfloat16),
                v_all[index],
                preferred_element_type=jnp.float32,
            )

        def widest(scores):
            return functools.reduce(
                jnp.maximum, [scores[:, at : at + HD] for at in range(0, keys, HD)]
            )

        for m in range(2):

            def chunk(step, carry, m=m):
                start = step * step_sources
                query = q_ref[pl.ds(start, step_sources), m].reshape(SAFE_CHUNK, HD)
                allowed = causal(start, SAFE_CHUNK, per, zh, keys)
                scores = jnp.where(allowed, scores_of(query, k_all[OWN + m]), -1e30)
                s_all[0] = scores
                peak[...] = widest(scores)
                for slot, index in enumerate(SOURCES[m]):

                    @pl.when(live_of(links_ref, place_ref, m, slot))
                    def _(slot=slot, index=index):
                        scores = scores_of(query, k_all[index])
                        s_all[slot + 1] = scores
                        peak[...] = jnp.maximum(peak[...], widest(scores))

                top = jnp.max(peak[...], axis=1, keepdims=True)
                peak[...] = jnp.broadcast_to(top, (SAFE_CHUNK, HD))
                acc[...] = sums_of(0, OWN + m)
                for slot, index in enumerate(SOURCES[m]):

                    @pl.when(live_of(links_ref, place_ref, m, slot))
                    def _(slot=slot, index=index):
                        acc[...] += sums_of(slot + 1, index)

                result = (acc[:, :HD] / acc[:, HD:]).astype(jnp.bfloat16)
                o_ref[pl.ds(start, step_sources), m] = result.reshape(step_sources, per, HD)
                return carry

            lax.fori_loop(0, q_ref.shape[0] // step_sources, chunk, 0)


def call(kernel, outputs, scratch, flops, scalars, arrays):
    smem = pl.BlockSpec(memory_space=pltpu.SMEM)
    vmem = pl.BlockSpec(memory_space=pltpu.VMEM)
    return pl.pallas_call(
        kernel,
        out_shape=outputs,
        in_specs=[smem] * len(scalars) + [vmem] * len(arrays),
        out_specs=jax.tree.map(lambda _: vmem, outputs),
        scratch_shapes=scratch,
        compiler_params=pltpu.CompilerParams(vmem_limit_bytes=44 * 1024 * 1024),
        cost_estimate=pl.CostEstimate(flops=flops, bytes_accessed=2**20, transcendentals=0),
    )(*scalars, *arrays)


def pack_pairs(keys, values):
    resp, near, width = keys.shape
    output = jax.ShapeDtypeStruct((resp // 2 * width // HD, 2, 2, near, HD), jnp.bfloat16)
    return pl.pallas_call(
        pack_pairs_kernel,
        out_shape=output,
        in_specs=[pl.BlockSpec(memory_space=pltpu.VMEM)] * 2,
        out_specs=pl.BlockSpec(memory_space=pltpu.VMEM),
        compiler_params=pltpu.CompilerParams(vmem_limit_bytes=60 * 1024 * 1024),
    )(keys, values)


def join(mine, other):
    shape = mine.shape[:2] + (2 * mine.shape[2], HD)
    output = jax.ShapeDtypeStruct(shape, jnp.bfloat16)
    return call(join_kernel, output, [], 60 * 10**9, (), (mine, other))


def pack_queries(queries, groups):
    resp, near, width = queries.shape
    shape = (resp // 2 * groups, 2, near * width // groups // HD, HD)
    output = jax.ShapeDtypeStruct(shape, jnp.bfloat16)
    return call(pack_queries_kernel, output, [], 10**6, (), (queries,))


def attend_early(links, place, query, *blocks):
    output = jax.ShapeDtypeStruct(query.shape[:3] + (2 * HD,), jnp.float32)
    return call(early_kernel, output, [], 4 * 10**9, (links, place), (query,) + blocks)


def attend_late(links, place, query, early, *blocks):
    keys = blocks[0].shape[2]
    output = jax.ShapeDtypeStruct(query.shape, jnp.bfloat16)
    scratch = [
        pltpu.VMEM((12, keys, HD), jnp.bfloat16),
        pltpu.VMEM((12, keys, 2 * HD), jnp.bfloat16),
        pltpu.VMEM((SLOTS + 1, SAFE_CHUNK, keys), jnp.float32),
        pltpu.VMEM((SAFE_CHUNK, HD), jnp.float32),
        pltpu.VMEM((SAFE_CHUNK, 2 * HD), jnp.float32),
        pltpu.VMEM((8, HD), jnp.float32),
    ]
    return call(late_kernel, output, scratch, 6 * 10**9, (links, place), (query, early) + blocks)


def ring(value, by, keep=lambda h: True):
    pairs = [(z, (z + by) % 16) for z in range(16) if keep(z % 8)]
    return lax.ppermute(value, ("zh", "h"), pairs)


def along(value, by):
    return ring(value, by, lambda h: h + by < 8)


def across(value, by):
    return lax.ppermute(value, "x", [(x, (x + by) % 4) for x in range(4)])


def local(queries, keys, values, links):
    resp, near, width = queries.shape
    groups = keys.shape[2] // HD
    repeat = width // keys.shape[2]
    x, zh, h = lax.axis_index("x"), lax.axis_index("zh"), lax.axis_index("h")

    with jax.named_scope("key_value_exchange"):
        own = pack_pairs(keys, values)
        own = lax.all_to_all(own, PLANE, split_axis=0, concat_axis=0, tiled=True)
        own = own.transpose(1, 2, 0, 3, 4).reshape(2, 2, 4 * groups * near, HD)
        own = join(own, ring(own, 8))
    with jax.named_scope("query_exchange"):
        query = pack_queries(queries, groups)
        query = lax.all_to_all(query, PLANE, split_axis=0, concat_axis=0, tiled=True)
    place = jnp.stack([zh, h * resp + 2 * x]).astype(jnp.int32)
    with jax.named_scope("key_value_spread"):
        eight = along(own, 1)
        thirtytwo = ring(own, -4, lambda h: h < 4)
        sixteen = along(own, 2)
        two = across(jnp.where(x >= 2, eight, own), 2)
        one = across(jnp.where(x >= 3, eight, own), 1)
    with jax.named_scope("attend"):
        links = links.T
        early = attend_early(links, place, query, own, eight)
        result = attend_late(links, place, query, early, own, one, two, eight, sixteen, thirtytwo)
    with jax.named_scope("return_exchange"):
        result = lax.all_to_all(result, PLANE, split_axis=0, concat_axis=0, tiled=True)
        result = result.reshape(4, groups, 2, repeat, near, HD).transpose(0, 2, 4, 1, 3, 5)
        return result.reshape(resp, near, width)


def solution(mesh):
    fine = Mesh(mesh.devices.reshape(4, 2, 4, 2, 8), ("x", "zh", "y", "c", "h"))
    placed = P("h", ("x", "zh", "y", "c"), None)
    return jax.shard_map(
        local, mesh=fine, in_specs=(placed, placed, placed, P()), out_specs=placed, check_vma=False
    )
```
